256 devices in a mesh: expert: 8 (over z), ray: 32 (over x, y, core).
Axes of the slice: x: 4, y: 4, z: 8, core: 2. Of those that a mesh axis runs over, the one named last changes fastest.
Arguments:
- features: bfloat16 [4096, 128, 256], P(('expert', 'ray')), may hold values from -6 to 6
- routes: int32 [4096, 128, 1], P(('expert', 'ray')), may hold values from 0 to 15; in each aligned block of 2048 rows (0 to 2047, 2048 to 4095, ..., all dimensions but the last counted through in order) at most 256 rows name the same one
- gate_values: bfloat16 [4096, 128], P(('expert', 'ray')), may hold values from 0.29882812 to 1
- deltas: float32 [4096, 128], P(('expert', 'ray')), may hold values from 0.004 to 0.04
- target: float32 [3, 4096], P(None, ('expert', 'ray')), may hold values from 0 to 1
- w_hidden: bfloat16 [16, 4, 256, 256], P('expert', None, 'ray'), may hold values from -0.375 to 0.375
- b_hidden: bfloat16 [16, 4, 256], P('expert', None, 'ray'), may hold values from -1.5 to 1.5
- w_head: bfloat16 [16, 4, 256], P('expert', None, 'ray'), may hold values from -0.375 to 0.375
Outputs:
- rendered: float32 [3, 4096], P(None, ('expert', 'ray'))
- grad_hidden: float32 [16, 4, 256, 256], P('expert', None, 'ray')
- grad_bias: float32 [16, 4, 256], P('expert', None, 'ray')
- grad_head: float32 [16, 4, 256], P('expert', None, 'ray')
The draws below stay inside these ranges and needn't reach their ends.
Inputs may be any that keep to these rules, and one draw needn't show every extreme that they name: `routes`: among the rows of one device (aligned blocks of 2048 samples), no expert is named by more than 256 samples, a bound that some block reaches.
All inputs are finite; a program needn't handle non-finite values.
Results may differ from the reference program's by a relative error of at most 0.0035.
Values may be sent and summed in bfloat16 or wider, within the bound.
No kernel may reach another device: no remote copies, remote signals or barrier semaphores. Data moves between devices by JAX's collectives and lax.ppermute only.
A program may use at most 128 MiB of HBM per device.

```python
import math
from functools import partial
import jax
import jax.numpy as jnp
import numpy as np
from jax import lax

D = 256
S = 128
LAYERS = 4
RAYS_DEV = 16
EXPERTS = 16
RAYS = 4096
CAP = 256
N_EXPERT = 8
N_RAY = 32


def levels(stream_key, shape, shards, smallest, largest):
    def one(dim, shards_of):
        steps = jax.random.uniform(jax.random.fold_in(jax.random.fold_in(stream_key, 6), dim), (shards_of,), jnp.float32, smallest / len(shards), largest / len(shards))
        return jnp.repeat(jnp.exp(steps), shape[dim] // shards_of).reshape((-1,) + (1,) * (len(shape) - dim - 1))

    factor_of = one(*shards[0])
    for cut in shards[1:]:
        factor_of = factor_of * one(*cut)
    return factor_of


def shared_out(own_key, own, number, rows, count, top, limit, lean):
    ranking = jax.random.permutation(own_key, count)
    crowded, ordinary = shares(count, rows * top, limit, lean, True), shares(count, rows * top, limit, lean, False)
    places = jnp.arange(count)

    def named(tallies, rotation):
        used = int((tallies > 0).sum())
        fixed = max(1, used // 4)
        passed = fixed + (places - fixed + rotation * (used - fixed)) % max(1, count - fixed)
        return jnp.zeros((count,), jnp.int32).at[ranking[jnp.where(places < fixed, places, passed)]].set(jnp.asarray(tallies, jnp.int32))

    tallies = jnp.where(number % 4 == 0, named(crowded, number // 4), named(ordinary, number - number // 4 - 1))
    mixed = jax.random.permutation(jax.random.fold_in(own, 3), count)
    source_of, receiver = mixed[0:count // 2 * 2:2], mixed[1:count // 2 * 2:2]
    slack = jnp.minimum(tallies[source_of] - 1, limit - tallies[receiver]) // 2
    slack = jnp.where((source_of == ranking[0]) | (receiver == ranking[0]) | (tallies[receiver] == 0), 0, jnp.maximum(slack, 0))
    passed = jax.random.randint(jax.random.fold_in(own, 4), (count // 2,), 0, 1 << 20) % (slack + 1)
    tallies = tallies.at[source_of].add(-passed).at[receiver].add(passed)
    labels = jnp.searchsorted(jnp.cumsum(tallies), jnp.arange(rows * top), side="right").astype(jnp.int32)
    listing = labels.reshape(top, rows).T
    listing = listing[jax.random.permutation(jax.random.fold_in(own, 1), rows)]
    rotation = jax.random.randint(jax.random.fold_in(own, 2), (rows, 1), 0, top)
    return jnp.take_along_axis(listing, (jnp.arange(top)[None, :] + rotation) % top, axis=1)


def shares(count, total, limit, lean, full):
    portions = [(1 << 20) // math.isqrt(grade ** lean) + 1 for grade in range(1, count + 1)]
    largest = limit if full else min(limit, max(-(-total // count), total * portions[0] // sum(portions)))
    least = 1 if total - largest >= count - 1 else 0
    counts, surplus = [largest] + [least] * (count - 1), total - largest - least * (count - 1)
    while surplus > 0:
        candidates = [i for i in range(1, count) if counts[i] < largest] or [i for i in range(1, count) if counts[i] < limit]
        pool, left = sum([portions[i] for i in candidates]), surplus
        for i in candidates:
            addition = min(limit - counts[i], max(1, left * portions[i] // pool), surplus)
            counts[i] = counts[i] + addition
            surplus = surplus - addition
    return np.array(counts)


def noise(rng, dims, width, most, cuts=(), kind=jnp.bfloat16):
    drawn = jax.random.normal(rng, dims, jnp.float32) * width
    if len(cuts) > 0:
        drawn = levels(rng, dims, cuts, -0.22, 0.18) * drawn
    return jnp.clip(drawn, min=-most, max=most).astype(kind)


def setup_inputs(seed: int = 0) -> dict:
    streams_of = jax.random.split(jax.random.key(seed), 9)
    features = noise(streams_of[0], (RAYS, S, D), 1.0, 6.0, ((0, 256),))
    routes_keys = jax.random.split(jax.random.fold_in(streams_of[1], 1), RAYS * S // (RAYS_DEV * S))
    routes_turns = jax.random.permutation(jax.random.fold_in(streams_of[1], 3), RAYS * S // (RAYS_DEV * S))
    routes = jax.vmap(lambda own, number: shared_out(jax.random.fold_in(streams_of[1], 2), own, number, RAYS_DEV * S, EXPERTS, 1, CAP, 2))(routes_keys, routes_turns).reshape((RAYS, S, 1))
    gate_values = jnp.clip(0.29882812 + 0.7011719 * jax.random.uniform(streams_of[2], (RAYS, S), jnp.float32) ** levels(streams_of[2], (RAYS, S), ((0, 256),), -0.2, 0.2), 0.29882812, 1.0).astype(jnp.bfloat16)
    deltas = jnp.clip(jnp.exp(math.log(0.04) - 2.30258502 * jax.random.uniform(streams_of[3], (RAYS, S), jnp.float32) ** levels(streams_of[3], (RAYS, S), ((0, 256),), -0.2, 0.2)), 0.004, 0.04)
    target = jnp.clip(1.0 * jax.random.uniform(streams_of[4], (3, RAYS), jnp.float32) ** levels(streams_of[4], (3, RAYS), ((1, 256),), -0.2, 0.2), 0.0, 1.0)
    w_hidden = noise(streams_of[5], (EXPERTS, LAYERS, D, D), D ** -0.5, 0.375, ((0, 8), (2, 32)))
    b_hidden = noise(streams_of[6], (EXPERTS, LAYERS, D), 0.3, 1.5, ((0, 8), (2, 32)))
    w_head = noise(streams_of[7], (EXPERTS, 4, D), D ** -0.5, 0.375, ((0, 8), (2, 32)))
    return {"features": features, "routes": routes, "gate_values": gate_values, "deltas": deltas, "target": target, "w_hidden": w_hidden, "b_hidden": b_hidden, "w_head": w_head}


def gelu_tanh(value):
    return jax.nn.gelu(value, approximate=True)

def gelu_slope(value):
    return jax.vjp(gelu_tanh, value)[1](jnp.ones_like(value))[0]

def composite(gated_out, deltas):
    density = jax.nn.softplus(gated_out[0])
    radiance = jax.nn.sigmoid(gated_out[1:])
    optical = density * deltas
    before = jnp.cumsum(optical, axis=1) - optical
    weight = jnp.exp(-before) * (1.0 - jnp.exp(-optical))
    return lax.optimization_barrier(jnp.sum(weight[None] * radiance, axis=2))

def expert_forward(w_layers, b_layers, head, inputs):
    hidden = inputs
    activations = [hidden]
    pre_acts = []
    for layer in range(w_layers.shape[0]):
        pre_act = jnp.dot(hidden, w_layers[layer], preferred_element_type=jnp.float32) + b_layers[layer].astype(jnp.float32)
        pre_acts.append(pre_act)
        hidden = gelu_tanh(pre_act).astype(jnp.bfloat16)
        activations.append(hidden)
    output = jnp.dot(head, hidden.T, preferred_element_type=jnp.float32)
    return (activations, pre_acts, output)

def expert_grads(w_layers, b_layers, head, inputs, cotangent):
    activations, pre_acts, output = expert_forward(w_layers, b_layers, head, inputs)
    grad_head = jnp.dot(cotangent, activations[-1], preferred_element_type=jnp.float32)
    grad_hidden = jnp.dot(cotangent.T, head, preferred_element_type=jnp.float32)
    layer_total = w_layers.shape[0]
    weight_list = [None] * layer_total
    shift_list = [None] * layer_total
    for layer in range(layer_total - 1, -1, -1):
        grad_pre = (grad_hidden * gelu_slope(pre_acts[layer])).astype(jnp.bfloat16)
        weight_list[layer] = jnp.dot(activations[layer].T, grad_pre, preferred_element_type=jnp.float32)
        shift_list[layer] = lax.optimization_barrier(jnp.sum(grad_pre, axis=0, dtype=jnp.float32))
        if layer > 0:
            grad_hidden = jnp.dot(grad_pre, w_layers[layer].T, preferred_element_type=jnp.float32)
    return (jnp.stack(weight_list), jnp.stack(shift_list), grad_head)

def reference(features, routes, gate_values, deltas, target, w_hidden, b_hidden, w_head):
    devices = N_EXPERT * N_RAY
    row_count = RAYS_DEV * S
    route_flat = routes.reshape(devices, row_count)
    onehot = (route_flat[:, :, None] == jnp.arange(EXPERTS, dtype=jnp.int32)[None, None, :]).astype(jnp.int32)
    slot_pos = lax.optimization_barrier(jnp.sum(onehot * (jnp.cumsum(onehot, axis=1) - 1), axis=2))
    device_ids = jnp.arange(devices, dtype=jnp.int32)[:, None]
    slot_index = (route_flat * (devices * CAP) + device_ids * CAP + slot_pos).reshape(-1).astype(jnp.int32)
    buffer = jnp.zeros((EXPERTS * devices * CAP, D), features.dtype)
    buffer = buffer.at[slot_index].set(features.reshape(-1, D)).reshape(EXPERTS, devices * CAP, D)

    def forward_one(operands):
        return expert_forward(*operands)[2]
    outputs = lax.map(forward_one, (w_hidden, b_hidden, w_head, buffer))
    raw_out = outputs.transpose(0, 2, 1).reshape(-1, 4)[slot_index]
    gate_float = gate_values.astype(jnp.float32)
    gated_out = gate_float[None] * raw_out.T.reshape(4, RAYS, S)
    rendered, pullback = jax.vjp(partial(composite, deltas=deltas), gated_out)
    grad_gated = pullback(rendered - target)[0]
    cotangent = (gate_float[None] * grad_gated).astype(jnp.bfloat16).reshape(4, -1)
    cot_slots = jnp.zeros((4, EXPERTS * devices * CAP), cotangent.dtype)
    cot_slots = cot_slots.at[:, slot_index].set(cotangent).reshape(4, EXPERTS, devices * CAP).transpose(1, 0, 2)

    def backward_one(operands):
        return expert_grads(*operands)
    grad_weight, grad_shift, grad_head = lax.map(backward_one, (w_hidden, b_hidden, w_head, buffer, cot_slots))
    return (rendered, grad_weight, grad_shift, grad_head)
```

```python
import jax
import jax.numpy as jnp
import numpy as np
from jax import lax
from jax.experimental import pallas as pl
from jax.experimental.pallas import tpu as pltpu
from jax.sharding import Mesh
from jax.sharding import PartitionSpec as P

BF = jnp.bfloat16
F32 = jnp.float32
I32 = jnp.int32
K0 = float(np.sqrt(2.0 / np.pi))
K1 = 0.044715
EXPERTS = 16
CAP = 256
ROWS = 2048
RAYS = 16
S = 128
D = 256
LAYERS = 4
CH = 72


def dot(a, b, dims, **kw):
    return lax.dot_general(a, b, (dims, ((), ())), preferred_element_type=F32, **kw)


def params(mb=48):
    return pltpu.CompilerParams(vmem_limit_bytes=mb * 2**20)


def prep_kernel(w_ref, b_ref, h_ref, out_ref):
    eye = (
        lax.broadcasted_iota(I32, (8, 128), 0) == lax.broadcasted_iota(I32, (8, 128), 1)
    ).astype(F32)
    for e in range(2):
        parts = []
        for l in range(LAYERS):
            rows = w_ref[e, l].astype(F32)
            parts += [rows[:, :128], rows[:, 128:]]
        extra = jnp.concatenate([b_ref[e].astype(F32), h_ref[e].astype(F32)], axis=0)
        parts.append(dot(extra.astype(BF), eye.astype(BF), ((0,), (0,))))
        out_ref[e] = jnp.concatenate(parts, axis=0).astype(BF)


def prep(w, b, h):
    return pl.pallas_call(
        prep_kernel, out_shape=jax.ShapeDtypeStruct((2, CH, 128), BF), compiler_params=params()
    )(w, b, h)


def pack_kernel(route_ref, x_ref, out_ref, slot_ref):
    @pl.when(pl.program_id(0) == 0)
    def _():
        route = route_ref[...]
        member = jnp.concatenate([(route == e).astype(F32) for e in range(EXPERTS)], axis=0)
        member16 = member.astype(BF)
        row = lax.broadcasted_iota(I32, (256, 256), 0)
        col = lax.broadcasted_iota(I32, (256, 256), 1)
        before = ((row // RAYS == col // RAYS) & (col < row)).astype(BF)
        lane_r = lax.broadcasted_iota(I32, (128, 128), 0)
        lane_c = lax.broadcasted_iota(I32, (128, 128), 1)
        upto = (lane_r <= lane_c).astype(BF)
        within = dot(member16, upto, ((1,), (0,)))
        earlier = dot(before, member16, ((1,), (0,)))
        earlier = dot(earlier.astype(BF), jnp.ones((128, 128), BF), ((1,), (0,)))
        rank = within + earlier - 1.0
        slot = jnp.zeros((RAYS, S), F32)
        for e in range(EXPERTS):
            part = slice(e * RAYS, (e + 1) * RAYS)
            slot = slot + member[part] * (rank[part] + float(e * CAP))
        slot_ref[...] = slot.astype(I32)

    step = pl.program_id(0)
    place = lax.broadcasted_iota(I32, (CAP, S), 0)
    for half in range(2):
        base = (step * 2 + half) * CAP
        hot = jnp.concatenate(
            [
                jnp.where(slot_ref[j : j + 1, :] - base == place, 1.0, 0.0).astype(BF)
                for j in range(RAYS)
            ],
            axis=1,
        )
        out_ref[half] = dot(hot, x_ref[...], ((1,), (0,))).astype(BF)


def pack(route, x):
    return pl.pallas_call(
        pack_kernel,
        grid=(8,),
        in_specs=[
            pl.BlockSpec((RAYS, S), lambda i: (0, 0)),
            pl.BlockSpec((ROWS, D), lambda i: (0, 0)),
        ],
        out_specs=[
            pl.BlockSpec((2, CAP, D), lambda i: (i, 0, 0)),
            pl.BlockSpec((RAYS, S), lambda i: (0, 0)),
        ],
        out_shape=[
            jax.ShapeDtypeStruct((EXPERTS, CAP, D), BF),
            jax.ShapeDtypeStruct((RAYS, S), I32),
        ],
        compiler_params=params(),
    )(route, x)


def forward_kernel(core_ref, g_ref, x_ref, h_ref, slope_ref, out_ref, w_ref, v_ref):
    @pl.when(pl.program_id(0) == 0)
    def _():
        for l in range(LAYERS):
            for half in range(2):
                at = (l * 2 + half) * 8
                part = g_ref[:, 0, at : at + 8, :].astype(F32).reshape(D, 128)
                w_ref[l, :, half * 128 : half * 128 + 128] = part.astype(BF)
        extra = g_ref[:, 0, 64:72, :].astype(F32).reshape(D, 128)
        v_ref[...] = extra.T[0:8]

    hidden = x_ref[...].reshape(2 * CAP, D)
    for l in range(LAYERS):
        pre = dot(hidden, w_ref[l], ((1,), (0,))) + v_ref[l : l + 1, :]
        square = pre * pre
        t = jnp.tanh(pre * (K0 + (K0 * K1) * square))
        cdf = 0.5 + 0.5 * t
        value = pre * cdf
        slope_ref[l] = cdf + value * (1.0 - t) * (K0 + (3.0 * K0 * K1) * square)
        hidden = value.astype(BF)
        h_ref[l] = hidden
    out = dot(v_ref[...].astype(BF), hidden, ((1,), (1,))).astype(BF).astype(F32)
    for s in range(2):
        at = s * CAP
        out_ref[s, 0:4, :] = out[4:8, at : at + 128]
        out_ref[s, 4:8, :] = out[4:8, at + 128 : at + 256]


def forward(core, gathered, x):
    return pl.pallas_call(
        forward_kernel,
        grid_spec=pltpu.PrefetchScalarGridSpec(
            num_scalar_prefetch=1,
            grid=(8,),
            in_specs=[
                pl.BlockSpec((32, 1, CH, 128), lambda i, c: (0, c[0], 0, 0)),
                pl.BlockSpec((2, CAP, D), lambda i, c: (i, 0, 0)),
            ],
            out_specs=[
                pl.BlockSpec((LAYERS, 2 * CAP, D), lambda i, c: (0, i, 0)),
                pl.BlockSpec((LAYERS, 2 * CAP, D), lambda i, c: (0, i, 0)),
                pl.BlockSpec((2, 8, 128), lambda i, c: (i, 0, 0)),
                pl.BlockSpec((LAYERS, D, D), lambda i, c: (0, 0, 0)),
                pl.BlockSpec((8, D), lambda i, c: (0, 0)),
            ],
        ),
        out_shape=[
            jax.ShapeDtypeStruct((LAYERS, EXPERTS * CAP, D), BF),
            jax.ShapeDtypeStruct((LAYERS, EXPERTS * CAP, D), F32),
            jax.ShapeDtypeStruct((EXPERTS, 8, 128), F32),
            jax.ShapeDtypeStruct((LAYERS, D, D), BF),
            jax.ShapeDtypeStruct((8, D), F32),
        ],
        compiler_params=params(),
    )(core, gathered, x)


def composite_kernel(table_ref, slot_ref, gate_ref, delta_ref, target_ref, rend_ref, cot_ref):
    table = jnp.concatenate(
        [
            jnp.concatenate([table_ref[:, c, :], table_ref[:, 4 + c, :]], axis=1)
            for c in range(4)
        ],
        axis=0,
    ).astype(BF)
    slot = slot_ref[...]
    place = lax.broadcasted_iota(I32, (CAP, S), 0)
    expert = lax.broadcasted_iota(I32, (EXPERTS, S), 0)
    hots, members, rows = [], [], []
    for j in range(RAYS):
        at = slot[j : j + 1, :]
        hot = jnp.where((at & (CAP - 1)) == place, 1.0, 0.0).astype(BF)
        member = jnp.where(lax.shift_right_logical(at, 8) == expert, 1.0, 0.0)
        found = dot(table, hot, ((1,), (0,)))
        rows.append(
            [
                jnp.sum(found[c * 16 : c * 16 + 16] * member, axis=0, keepdims=True)
                for c in range(4)
            ]
        )
        hots.append(hot)
        members.append(member)
    raw = [jnp.concatenate([rows[j][c] for j in range(RAYS)], axis=0) for c in range(4)]
    gate = gate_ref[...].astype(F32)
    delta = delta_ref[...]
    gated = [gate * r for r in raw]
    lane_r = lax.broadcasted_iota(I32, (128, 128), 0)
    lane_c = lax.broadcasted_iota(I32, (128, 128), 1)
    earlier = (lane_r < lane_c).astype(F32)
    later = (lane_r > lane_c).astype(F32)
    g0 = gated[0]
    density = jnp.maximum(g0, 0.0) + jnp.log1p(jnp.exp(-jnp.abs(g0)))
    radiance = [jax.nn.sigmoid(g) for g in gated[1:]]
    optical = density * delta
    before = dot(optical, earlier, ((1,), (0,)), precision=lax.Precision.HIGHEST)
    reach = jnp.exp(-before)
    passed = jnp.exp(-optical)
    weight = reach * (1.0 - passed)
    eye = lax.broadcasted_iota(I32, (RAYS, RAYS), 0) == lax.broadcasted_iota(I32, (RAYS, RAYS), 1)
    q = jnp.zeros((RAYS, S), F32)
    grads = [None]
    for c in range(3):
        rendered = jnp.sum(weight * radiance[c], axis=1, keepdims=True)
        goal = jnp.sum(jnp.where(eye, target_ref[c : c + 1, :], 0.0), axis=1, keepdims=True)
        rend_ref[c : c + 1, :] = jnp.sum(jnp.where(eye, rendered, 0.0), axis=0, keepdims=True)
        diff = rendered - goal
        q = q + diff * radiance[c]
        grads.append(diff * weight * radiance[c] * (1.0 - radiance[c]))
    push = dot(q * weight, later, ((1,), (0,)), precision=lax.Precision.HIGHEST)
    grads[0] = (q * reach * passed - push) * delta * jax.nn.sigmoid(g0)
    cots = [(gate * g).astype(BF).astype(F32) for g in grads]
    total = jnp.zeros((64, CAP), F32)
    for j in range(RAYS):
        spread = jnp.concatenate([cots[c][j : j + 1, :] * members[j] for c in range(4)], axis=0)
        total = total + dot(spread.astype(BF), hots[j], ((1,), (1,)))
    for c in range(4):
        cot_ref[:, c, :] = total[c * 16 : c * 16 + 16, :128]
        cot_ref[:, 4 + c, :] = total[c * 16 : c * 16 + 16, 128:]


def composite(table, slot, gate, delta, target):
    return pl.pallas_call(
        composite_kernel,
        out_shape=[
            jax.ShapeDtypeStruct((3, RAYS), F32),
            jax.ShapeDtypeStruct((EXPERTS, 8, 128), F32),
        ],
        compiler_params=params(),
    )(table, slot, gate, delta, target)


def backward_kernel(cot_ref, x_ref, h_ref, slope_ref, w_ref, v_ref, out_ref, gw_ref, gv_ref):
    step = pl.program_id(0)

    @pl.when(step == 0)
    def _():
        gw_ref[...] = jnp.zeros_like(gw_ref)
        gv_ref[...] = jnp.zeros_like(gv_ref)

    cot = jnp.concatenate(
        [cot_ref[0, 0:4], cot_ref[0, 4:8], cot_ref[1, 0:4], cot_ref[1, 4:8]], axis=1
    ).astype(BF)
    head = v_ref[4:8, :].astype(BF)
    gv_ref[4:8, :] += dot(cot, h_ref[LAYERS - 1], ((1,), (0,)))
    grad = dot(cot, head, ((0,), (0,)))
    ones = jnp.ones((8, 2 * CAP), BF)
    for l in range(LAYERS - 1, -1, -1):
        grad_pre = (grad * slope_ref[l]).astype(BF)
        below = h_ref[l - 1] if l > 0 else x_ref[...].reshape(2 * CAP, D)
        gw_ref[l] += dot(below, grad_pre, ((0,), (0,)))
        gv_ref[l : l + 1, :] += dot(ones, grad_pre, ((1,), (0,)))[0:1]
        if l > 0:
            grad = dot(grad_pre, w_ref[l], ((1,), (1,)))

    @pl.when(step == pl.num_programs(0) - 1)
    def _():
        for l in range(LAYERS):
            for half in range(2):
                at = (l * 2 + half) * 8
                part = gw_ref[l, :, half * 128 : half * 128 + 128]
                out_ref[:, at : at + 8, :] = part.reshape(32, 8, 128)
        extra = jnp.concatenate([gv_ref[...], jnp.zeros((120, D), F32)], axis=0)
        out_ref[:, 64:72, :] = extra.T.reshape(32, 8, 128)


def backward(cot, x, h, slope, w, v):
    return pl.pallas_call(
        backward_kernel,
        grid=(8,),
        in_specs=[
            pl.BlockSpec((2, 8, 128), lambda i: (i, 0, 0)),
            pl.BlockSpec((2, CAP, D), lambda i: (i, 0, 0)),
            pl.BlockSpec((LAYERS, 2 * CAP, D), lambda i: (0, i, 0)),
            pl.BlockSpec((LAYERS, 2 * CAP, D), lambda i: (0, i, 0)),
            pl.BlockSpec((LAYERS, D, D), lambda i: (0, 0, 0)),
            pl.BlockSpec((8, D), lambda i: (0, 0)),
        ],
        out_specs=pl.BlockSpec((32, CH, 128), lambda i: (0, 0, 0)),
        out_shape=jax.ShapeDtypeStruct((32, CH, 128), F32),
        scratch_shapes=[pltpu.VMEM((LAYERS, D, D), F32), pltpu.VMEM((8, D), F32)],
        compiler_params=params(),
    )(cot, x, h, slope, w, v)


def finish_kernel(parts_ref, gw_ref, gb_ref, gh_ref):
    for e in range(2):
        total = parts_ref[0, e]
        for j in range(1, 16):
            total = total + parts_ref[j, e]
        for l in range(LAYERS):
            at = l * 16
            gw_ref[e, l] = jnp.concatenate([total[at : at + 8], total[at + 8 : at + 16]], axis=1)
        extra = jnp.concatenate([total[64:72], jnp.zeros((120, 128), F32)], axis=0).T
        gb_ref[e] = extra[0:4, 0:8]
        gh_ref[e] = extra[4:8, 0:8]


def finish(parts):
    return pl.pallas_call(
        finish_kernel,
        out_shape=[
            jax.ShapeDtypeStruct((2, LAYERS, 8, D), F32),
            jax.ShapeDtypeStruct((2, LAYERS, 8), F32),
            jax.ShapeDtypeStruct((2, 4, 8), F32),
        ],
        compiler_params=params(),
    )(parts)


def local(features, routes, gate_values, deltas, target, w_hidden, b_hidden, w_head):
    core = lax.axis_index("c").astype(I32).reshape(1)
    shard = prep(w_hidden, b_hidden, w_head)
    gathered = lax.all_gather(shard, ("xy", "c"), axis=0, tiled=False)
    outgoing, slot = pack(routes.reshape(RAYS, S), features.reshape(ROWS, D))
    received = lax.all_to_all(outgoing, ("z", "c"), 0, 0, tiled=True)
    h, slope, out, w, v = forward(core, gathered, received)
    table = lax.all_to_all(out, ("z", "c"), 0, 0, tiled=True)
    rendered, cot = composite(table, slot, gate_values, deltas, target)
    cot = lax.all_to_all(cot, ("z", "c"), 0, 0, tiled=True)
    grads = backward(cot, received, h, slope, w, v)
    parts = lax.all_to_all(grads, ("xy", "c"), 0, 0, tiled=True)
    grad_w, grad_b, grad_h = finish(parts.reshape(16, 2, CH, 128))
    return rendered, grad_w, grad_b, grad_h


def solution(mesh):
    split = Mesh(mesh.devices.reshape(8, 16, 2), ("z", "xy", "c"))
    every = ("z", "xy", "c")
    ray = ("xy", "c")
    in_specs = (
        P(every, None, None),
        P(every, None, None),
        P(every, None),
        P(every, None),
        P(None, every),
        P("z", None, ray, None),
        P("z", None, ray),
        P("z", None, ray),
    )
    out_specs = (P(None, every), P("z", None, ray, None), P("z", None, ray), P("z", None, ray))
    return jax.shard_map(local, mesh=split, in_specs=in_specs, out_specs=out_specs, check_vma=False)
```

```python
from functools import partial

import jax
import jax.numpy as jnp
import numpy as np
from jax import lax
from jax.experimental import pallas as pl
from jax.experimental.pallas import tpu as pltpu
from jax.sharding import Mesh
from jax.sharding import PartitionSpec as P

BF = jnp.bfloat16
F32 = jnp.float32
I32 = jnp.int32
K0 = float(np.sqrt(2.0 / np.pi))
K1 = 0.044715
EXPERTS = 16
CAP = 256
ROWS = 2048
RAYS = 16
S = 128
D = 256
LAYERS = 4
SHIFTS = (0, 1, -1, 3, -3, 4, 2, -2)
GROUPS = ((0, 3), (3, 3), (6, 2))
CH = 72


def dot(a, b, dims, **kw):
    return lax.dot_general(a, b, (dims, ((), ())), preferred_element_type=F32, **kw)


def params(mb=16):
    return pltpu.CompilerParams(vmem_limit_bytes=mb * 2**20)


def prep_kernel(w_ref, b_ref, h_ref, out_ref):
    eye = lax.broadcasted_iota(I32, (8, 128), 0) == lax.broadcasted_iota(I32, (8, 128), 1)
    for e in range(2):
        parts = []
        for l in range(LAYERS):
            rows = w_ref[e, l].astype(F32)
            parts += [rows[:, :128], rows[:, 128:]]
        extra = jnp.concatenate([b_ref[e].astype(F32), h_ref[e].astype(F32)], axis=0)
        parts.append(dot(extra.astype(BF), eye.astype(F32).astype(BF), ((0,), (0,))))
        whole = jnp.concatenate(parts, axis=0).astype(BF)
        for d in range(32):
            out_ref[d, e] = whole


def prep(w, b, h):
    return pl.pallas_call(
        prep_kernel, out_shape=jax.ShapeDtypeStruct((32, 2, CH, 128), BF), compiler_params=params()
    )(w, b, h)


def unpack_kernel(g_ref, w_ref, v_ref):
    for e in range(2):
        for l in range(LAYERS):
            for half in range(2):
                at = (l * 2 + half) * 8
                part = g_ref[:, e, at : at + 8, :].astype(F32).reshape(D, 128)
                w_ref[e, l, :, half * 128 : half * 128 + 128] = part.astype(BF)
        extra = g_ref[:, e, 64:72, :].astype(F32).reshape(D, 128)
        v_ref[e] = extra.T[0:8]


def unpack(gathered):
    return pl.pallas_call(
        unpack_kernel,
        out_shape=[
            jax.ShapeDtypeStruct((2, LAYERS, D, D), BF),
            jax.ShapeDtypeStruct((2, 8, D), F32),
        ],
        compiler_params=params(),
    )(gathered)


def slots_of(route):
    member = jnp.concatenate([(route == e).astype(F32) for e in range(EXPERTS)], axis=0)
    member16 = member.astype(BF)
    row = lax.broadcasted_iota(I32, (256, 256), 0)
    col = lax.broadcasted_iota(I32, (256, 256), 1)
    before = ((row // RAYS == col // RAYS) & (col < row)).astype(F32).astype(BF)
    lane_r = lax.broadcasted_iota(I32, (128, 128), 0)
    lane_c = lax.broadcasted_iota(I32, (128, 128), 1)
    upto = (lane_r <= lane_c).astype(F32).astype(BF)
    within = dot(member16, upto, ((1,), (0,)))
    earlier = dot(before, member16, ((1,), (0,)))
    earlier = dot(earlier.astype(BF), jnp.ones((128, 128), BF), ((1,), (0,)))
    rank = within + earlier - 1.0
    slot = jnp.zeros((RAYS, S), F32)
    for e in range(EXPERTS):
        part = slice(e * RAYS, (e + 1) * RAYS)
        slot = slot + member[part] * (rank[part] + float(e * CAP))
    return slot.astype(I32)


def pack_block(plane, slot_ref, x_ref, out_ref):
    place = lax.broadcasted_iota(I32, (CAP, S), 0)
    for half in range(2):
        base = (plane * 2 + half) * CAP
        hot = jnp.concatenate(
            [
                jnp.where(slot_ref[j : j + 1, :] - base == place, 1.0, 0.0).astype(BF)
                for j in range(RAYS)
            ],
            axis=1,
        )
        out_ref[half] = dot(hot, x_ref[...], ((1,), (0,))).astype(BF)


def pack_kernel(shifts, first, *refs):
    if first:
        route_ref, x_ref, *out_refs, slot_ref = refs
        slot_ref[...] = slots_of(route_ref[...])
    else:
        slot_ref, x_ref, *out_refs = refs
    plane = lax.axis_index("z")
    for k, out_ref in zip(shifts, out_refs):
        pack_block((plane + (k & 7)) & 7, slot_ref, x_ref, out_ref)


def pack(shifts, first, route, x):
    out_shape = [jax.ShapeDtypeStruct((2, CAP, D), BF) for _ in shifts]
    if first:
        out_shape.append(jax.ShapeDtypeStruct((RAYS, S), I32))
    return pl.pallas_call(
        partial(pack_kernel, shifts, first), out_shape=out_shape, compiler_params=params()
    )(route, x)


def forward_kernel(n, olds_n, where_ref, *refs):
    x_refs, (w_ref, v_ref), refs = refs[:n], refs[n : n + 2], refs[n + 2 :]
    olds, (h_ref, slope_ref, out_ref) = refs[:olds_n], refs[olds_n:]
    hidden = [jnp.concatenate([r[e] for r in x_refs], axis=0) for e in range(2)]
    for l in range(LAYERS):
        for e in range(2):
            pre = dot(hidden[e], w_ref[e, l], ((1,), (0,))) + v_ref[e, l : l + 1, :]
            square = pre * pre
            t = jnp.tanh(pre * (K0 + (K0 * K1) * square))
            cdf = 0.5 + 0.5 * t
            value = pre * cdf
            slope_ref[e, l] = cdf + value * (1.0 - t) * (K0 + (3.0 * K0 * K1) * square)
            hidden[e] = value.astype(BF)
            h_ref[e, l] = hidden[e]
    at = 0
    for old in olds:
        for i in range(old.shape[0]):
            out_ref[where_ref[at]] = old[i]
            at += 1
    for e in range(2):
        out = dot(v_ref[e].astype(BF), hidden[e], ((1,), (1,))).astype(BF).astype(F32)
        for i in range(n):
            lo = i * CAP
            one = jnp.concatenate(
                [out[4:8, lo : lo + 128], out[4:8, lo + 128 : lo + CAP]], axis=0
            )
            if olds_n:
                out_ref[where_ref[at + i], e] = one
            else:
                out_ref[i, e] = one


def forward(where, xs, w, v, olds):
    n = len(xs)
    vmem = pl.BlockSpec(memory_space=pltpu.VMEM)
    return pl.pallas_call(
        partial(forward_kernel, n, len(olds)),
        in_specs=[pl.BlockSpec(memory_space=pltpu.SMEM)] + [vmem] * (n + 2 + len(olds)),
        out_shape=[
            jax.ShapeDtypeStruct((2, LAYERS, n * CAP, D), BF),
            jax.ShapeDtypeStruct((2, LAYERS, n * CAP, D), F32),
            jax.ShapeDtypeStruct((8 if olds else n, 2, 8, 128), F32),
        ],
        compiler_params=params(),
    )(where, *xs, w, v, *olds)


def composite_kernel(table_ref, slot_ref, gate_ref, delta_ref, target_ref, rend_ref, cot_ref):
    table = jnp.concatenate(
        [
            jnp.concatenate([table_ref[:, c, :], table_ref[:, 4 + c, :]], axis=1)
            for c in range(4)
        ],
        axis=0,
    ).astype(BF)
    slot = slot_ref[...]
    place = lax.broadcasted_iota(I32, (CAP, S), 0)
    expert = lax.broadcasted_iota(I32, (EXPERTS, S), 0)
    hots, members, rows = [], [], []
    for j in range(RAYS):
        at = slot[j : j + 1, :]
        hot = jnp.where((at & (CAP - 1)) == place, 1.0, 0.0).astype(BF)
        member = jnp.where(lax.shift_right_logical(at, 8) == expert, 1.0, 0.0)
        found = dot(table, hot, ((1,), (0,)))
        rows.append(
            [
                jnp.sum(found[c * 16 : c * 16 + 16] * member, axis=0, keepdims=True)
                for c in range(4)
            ]
        )
        hots.append(hot)
        members.append(member)
    raw = [jnp.concatenate([rows[j][c] for j in range(RAYS)], axis=0) for c in range(4)]
    gate = gate_ref[...].astype(F32)
    delta = delta_ref[...]
    gated = [gate * r for r in raw]
    lane_r = lax.broadcasted_iota(I32, (128, 128), 0)
    lane_c = lax.broadcasted_iota(I32, (128, 128), 1)
    earlier = (lane_r < lane_c).astype(F32)
    later = (lane_r > lane_c).astype(F32)
    g0 = gated[0]
    density = jnp.maximum(g0, 0.0) + jnp.log1p(jnp.exp(-jnp.abs(g0)))
    radiance = [jax.nn.sigmoid(g) for g in gated[1:]]
    optical = density * delta
    before = dot(optical, earlier, ((1,), (0,)), precision=lax.Precision.HIGHEST)
    reach = jnp.exp(-before)
    passed = jnp.exp(-optical)
    weight = reach * (1.0 - passed)
    eye = lax.broadcasted_iota(I32, (RAYS, RAYS), 0) == lax.broadcasted_iota(I32, (RAYS, RAYS), 1)
    q = jnp.zeros((RAYS, S), F32)
    grads = [None]
    for c in range(3):
        rendered = jnp.sum(weight * radiance[c], axis=1, keepdims=True)
        goal = jnp.sum(jnp.where(eye, target_ref[c : c + 1, :], 0.0), axis=1, keepdims=True)
        rend_ref[c : c + 1, :] = jnp.sum(jnp.where(eye, rendered, 0.0), axis=0, keepdims=True)
        diff = rendered - goal
        q = q + diff * radiance[c]
        grads.append(diff * weight * radiance[c] * (1.0 - radiance[c]))
    push = dot(q * weight, later, ((1,), (0,)), precision=lax.Precision.HIGHEST)
    grads[0] = (q * reach * passed - push) * delta * jax.nn.sigmoid(g0)
    cots = [(gate * g).astype(BF).astype(F32) for g in grads]
    total = jnp.zeros((64, CAP), F32)
    for j in range(RAYS):
        spread = jnp.concatenate([cots[c][j : j + 1, :] * members[j] for c in range(4)], axis=0)
        total = total + dot(spread.astype(BF), hots[j], ((1,), (1,)))
    for c in range(4):
        cot_ref[:, c, :] = total[c * 16 : c * 16 + 16, :128]
        cot_ref[:, 4 + c, :] = total[c * 16 : c * 16 + 16, 128:]


def composite(table, slot, gate, delta, target):
    return pl.pallas_call(
        composite_kernel,
        out_shape=[
            jax.ShapeDtypeStruct((3, RAYS), F32),
            jax.ShapeDtypeStruct((EXPERTS, 8, 128), F32),
        ],
        compiler_params=params(),
    )(table, slot, gate, delta, target)


def backward_kernel(flip, where_ref, cot_ref, w_ref, v_ref, *refs):
    count = len(GROUPS)
    x_refs, h_refs = refs[:8], refs[8 : 8 + count]
    slope_refs, out_ref = refs[8 + count : 8 + 2 * count], refs[-1]
    e = where_ref[9] ^ flip
    head = v_ref[e, 4:8, :].astype(BF)
    grads, grad_head = [], 0.0
    for (pos, n), h_ref in zip(GROUPS, h_refs):
        parts = []
        for i in range(n):
            one = cot_ref[where_ref[pos + i], e]
            parts += [one[0:4], one[4:8]]
        cot = jnp.concatenate(parts, axis=1).astype(BF)
        grad_head = grad_head + dot(cot, h_ref[e, LAYERS - 1], ((1,), (0,)))
        grads.append(dot(cot, head, ((0,), (0,))))
    shifts = [None] * LAYERS
    for l in range(LAYERS - 1, -1, -1):
        total, shift = 0.0, 0.0
        for g, (pos, n) in enumerate(GROUPS):
            grad_pre = (grads[g] * slope_refs[g][e, l]).astype(BF)
            if l > 0:
                below = h_refs[g][e, l - 1]
            else:
                below = jnp.concatenate([x_refs[pos + i][e] for i in range(n)], axis=0)
            total = total + dot(below, grad_pre, ((0,), (0,)))
            shift = shift + dot(jnp.ones((8, n * CAP), BF), grad_pre, ((1,), (0,)))[0:1]
            if l > 0:
                grads[g] = dot(grad_pre, w_ref[e, l], ((1,), (1,)))
        shifts[l] = shift
        for half in range(2):
            at = (l * 2 + half) * 8
            out_ref[:, at : at + 8, :] = total[:, half * 128 : half * 128 + 128].reshape(32, 8, 128)
    extra = jnp.concatenate(shifts + [grad_head, jnp.zeros((120, D), F32)], axis=0)
    out_ref[:, 64:72, :] = extra.T.reshape(32, 8, 128)


def backward(flip, where, cot, w, v, xs, hs, slopes):
    vmem = pl.BlockSpec(memory_space=pltpu.VMEM)
    return pl.pallas_call(
        partial(backward_kernel, flip),
        in_specs=[pl.BlockSpec(memory_space=pltpu.SMEM)] + [vmem] * (11 + 2 * len(GROUPS)),
        out_shape=jax.ShapeDtypeStruct((32, CH, 128), F32),
        compiler_params=params(),
    )(where, cot, w, v, *xs, *hs, *slopes)


def finish_kernel(parts_ref, gw_ref, gb_ref, gh_ref):
    for e in range(2):
        total = parts_ref[0, e]
        for j in range(1, 16):
            total = total + parts_ref[j, e]
        for l in range(LAYERS):
            at = l * 16
            gw_ref[e, l] = jnp.concatenate([total[at : at + 8], total[at + 8 : at + 16]], axis=1)
        extra = jnp.concatenate([total[64:72], jnp.zeros((120, 128), F32)], axis=0).T
        gb_ref[e] = extra[0:4, 0:8]
        gh_ref[e] = extra[4:8, 0:8]


def finish(parts):
    return pl.pallas_call(
        finish_kernel,
        out_shape=[
            jax.ShapeDtypeStruct((2, LAYERS, 8, D), F32),
            jax.ShapeDtypeStruct((2, LAYERS, 8), F32),
            jax.ShapeDtypeStruct((2, 4, 8), F32),
        ],
        compiler_params=params(),
    )(parts)


def along(x, k):
    return lax.ppermute(x, "z", [(i, (i + k) % 8) for i in range(8)])


def local(features, routes, gate_values, deltas, target, w_hidden, b_hidden, w_head):
    z = lax.axis_index("z").astype(I32)
    core = lax.axis_index("c").astype(I32)
    sources = (z - jnp.array(SHIFTS, I32)) & 7
    where = jnp.concatenate([sources, z.reshape(1), core.reshape(1)])
    x = features.reshape(ROWS, D)
    arrived = {}
    *blocks, slot = pack((4, 3, -3), True, routes.reshape(RAYS, S), x)
    for k, block in zip((4, 3, -3), blocks):
        arrived[k] = along(block, k)
    w_hidden, b_hidden, w_head, x, slot = lax.optimization_barrier(
        (w_hidden, b_hidden, w_head, x, slot)
    )
    copies = prep(w_hidden, b_hidden, w_head)
    copies, slot2, x2 = lax.optimization_barrier((copies, slot, x))
    blocks = pack((1, -1, 2, -2, 0), False, slot2, x2)
    for k, block in zip((1, -1, 2, -2), blocks):
        arrived[k] = along(block, k)
    arrived[0] = blocks[-1]
    gathered = lax.all_to_all(copies, ("xy", "c"), 0, 0, tiled=True)
    w, v = unpack(gathered)
    xs = [arrived[k] for k in SHIFTS]
    hs, slopes, olds = [], [], []
    for g, (pos, n) in enumerate(GROUPS):
        last = g == len(GROUPS) - 1
        h, slope, out = forward(where, xs[pos : pos + n], w, v, olds if last else [])
        hs.append(h)
        slopes.append(slope)
        olds.append(out)
    table = lax.all_to_all(out, "z", 0, 0, tiled=True)
    rendered, cot = composite(table.reshape(EXPERTS, 8, 128), slot, gate_values, deltas, target)
    cot = lax.all_to_all(cot.reshape(8, 2, 8, 128), "z", 0, 0, tiled=True)
    given = backward(1, where, cot, w, v, xs, hs, slopes)
    given = lax.ppermute(given, "c", [(0, 1), (1, 0)])
    grads = backward(0, where, cot, w, v, xs, hs, slopes) + given
    parts = lax.all_to_all(grads, ("xy", "c"), 0, 0, tiled=True)
    grad_w, grad_b, grad_h = finish(parts.reshape(16, 2, CH, 128))
    return rendered, grad_w, grad_b, grad_h


def solution(mesh):
    split = Mesh(mesh.devices.reshape(8, 16, 2), ("z", "xy", "c"))
    every = ("z", "xy", "c")
    ray = ("xy", "c")
    in_specs = (
        P(every, None, None),
        P(every, None, None),
        P(every, None),
        P(every, None),
        P(None, every),
        P("z", None, ray, None),
        P("z", None, ray),
        P("z", None, ray),
    )
    out_specs = (P(None, every), P("z", None, ray, None), P("z", None, ray), P("z", None, ray))
    return jax.shard_map(local, mesh=split, in_specs=in_specs, out_specs=out_specs, check_vma=False)
```

```python
from functools import partial

import jax
import jax.numpy as jnp
import numpy as np
from jax import lax
from jax.experimental import pallas as pl
from jax.experimental.pallas import tpu as pltpu
from jax.sharding import Mesh
from jax.sharding import PartitionSpec as P

BF = jnp.bfloat16
F32 = jnp.float32
I32 = jnp.int32
K0 = float(np.sqrt(2.0 / np.pi))
K1 = 0.044715
EXPERTS = 16
CAP = 256
ROWS = 2048
RAYS = 16
S = 128
D = 256
LAYERS = 4
SHIFTS = (0, 1, -1, 2, -2, 3, -3, 4)
GROUPS = ((0, 5), (5, 3))
CH = 72


def dot(a, b, dims, **kw):
    return lax.dot_general(a, b, (dims, ((), ())), preferred_element_type=F32, **kw)


def params(mb=16):
    return pltpu.CompilerParams(vmem_limit_bytes=mb * 2**20)


def prep_kernel(w_ref, b_ref, h_ref, out_ref):
    eye = lax.broadcasted_iota(I32, (8, 128), 0) == lax.broadcasted_iota(I32, (8, 128), 1)
    for e in range(2):
        parts = []
        for l in range(LAYERS):
            rows = w_ref[e, l].astype(F32)
            parts += [rows[:, :128], rows[:, 128:]]
        extra = jnp.concatenate([b_ref[e].astype(F32), h_ref[e].astype(F32)], axis=0)
        parts.append(dot(extra.astype(BF), eye.astype(F32).astype(BF), ((0,), (0,))))
        whole = jnp.concatenate(parts, axis=0).astype(BF)
        for d in range(32):
            out_ref[d, e] = whole


def prep(w, b, h):
    return pl.pallas_call(
        prep_kernel, out_shape=jax.ShapeDtypeStruct((32, 2, CH, 128), BF), compiler_params=params()
    )(w, b, h)


def unpack_kernel(g_ref, w_ref, v_ref):
    for e in range(2):
        for l in range(LAYERS):
            for half in range(2):
                at = (l * 2 + half) * 8
                part = g_ref[:, e, at : at + 8, :].astype(F32).reshape(D, 128)
                w_ref[e, l, :, half * 128 : half * 128 + 128] = part.astype(BF)
        extra = g_ref[:, e, 64:72, :].astype(F32).reshape(D, 128)
        v_ref[e] = extra.T[0:8]


def unpack(gathered):
    return pl.pallas_call(
        unpack_kernel,
        out_shape=[
            jax.ShapeDtypeStruct((2, LAYERS, D, D), BF),
            jax.ShapeDtypeStruct((2, 8, D), F32),
        ],
        compiler_params=params(),
    )(gathered)


def slots_of(route):
    member = jnp.concatenate([(route == e).astype(F32) for e in range(EXPERTS)], axis=0)
    member16 = member.astype(BF)
    row = lax.broadcasted_iota(I32, (256, 256), 0)
    col = lax.broadcasted_iota(I32, (256, 256), 1)
    before = ((row // RAYS == col // RAYS) & (col < row)).astype(F32).astype(BF)
    lane_r = lax.broadcasted_iota(I32, (128, 128), 0)
    lane_c = lax.broadcasted_iota(I32, (128, 128), 1)
    upto = (lane_r <= lane_c).astype(F32).astype(BF)
    within = dot(member16, upto, ((1,), (0,)))
    earlier = dot(before, member16, ((1,), (0,)))
    earlier = dot(earlier.astype(BF), jnp.ones((128, 128), BF), ((1,), (0,)))
    rank = within + earlier - 1.0
    slot = jnp.zeros((RAYS, S), F32)
    for e in range(EXPERTS):
        part = slice(e * RAYS, (e + 1) * RAYS)
        slot = slot + member[part] * (rank[part] + float(e * CAP))
    return slot.astype(I32)


def pack_block(plane, slot_ref, x_ref, out_ref):
    place = lax.broadcasted_iota(I32, (CAP, S), 0)
    for half in range(2):
        base = (plane * 2 + half) * CAP
        hot = jnp.concatenate(
            [
                jnp.where(slot_ref[j : j + 1, :] - base == place, 1.0, 0.0).astype(BF)
                for j in range(RAYS)
            ],
            axis=1,
        )
        out_ref[half] = dot(hot, x_ref[...], ((1,), (0,))).astype(BF)


def pack_kernel(shifts, first, *refs):
    if first:
        route_ref, x_ref, *out_refs, slot_ref = refs
        slot_ref[...] = slots_of(route_ref[...])
    else:
        slot_ref, x_ref, *out_refs = refs
    plane = lax.axis_index("z")
    for k, out_ref in zip(shifts, out_refs):
        pack_block((plane + (k & 7)) & 7, slot_ref, x_ref, out_ref)


def pack(shifts, first, route, x):
    out_shape = [jax.ShapeDtypeStruct((2, CAP, D), BF) for _ in shifts]
    if first:
        out_shape.append(jax.ShapeDtypeStruct((RAYS, S), I32))
    return pl.pallas_call(
        partial(pack_kernel, shifts, first), out_shape=out_shape, compiler_params=params()
    )(route, x)


def forward_kernel(n, olds_n, where_ref, *refs):
    x_refs, (w_ref, v_ref), refs = refs[:n], refs[n : n + 2], refs[n + 2 :]
    olds, (h_ref, slope_ref, out_ref) = refs[:olds_n], refs[olds_n:]
    hidden = [jnp.concatenate([r[e] for r in x_refs], axis=0) for e in range(2)]
    for l in range(LAYERS):
        for e in range(2):
            pre = dot(hidden[e], w_ref[e, l], ((1,), (0,))) + v_ref[e, l : l + 1, :]
            square = pre * pre
            t = jnp.tanh(pre * (K0 + (K0 * K1) * square))
            cdf = 0.5 + 0.5 * t
            value = pre * cdf
            slope_ref[e, l] = cdf + value * (1.0 - t) * (K0 + (3.0 * K0 * K1) * square)
            hidden[e] = value.astype(BF)
            h_ref[e, l] = hidden[e]
    at = 0
    for old in olds:
        for i in range(old.shape[0]):
            out_ref[where_ref[at]] = old[i]
            at += 1
    for e in range(2):
        out = dot(v_ref[e].astype(BF), hidden[e], ((1,), (1,))).astype(BF).astype(F32)
        for i in range(n):
            lo = i * CAP
            one = jnp.concatenate(
                [out[4:8, lo : lo + 128], out[4:8, lo + 128 : lo + CAP]], axis=0
            )
            if olds_n:
                out_ref[where_ref[at + i], e] = one
            else:
                out_ref[i, e] = one


def forward(where, xs, w, v, olds):
    n = len(xs)
    vmem = pl.BlockSpec(memory_space=pltpu.VMEM)
    return pl.pallas_call(
        partial(forward_kernel, n, len(olds)),
        in_specs=[pl.BlockSpec(memory_space=pltpu.SMEM)] + [vmem] * (n + 2 + len(olds)),
        out_shape=[
            jax.ShapeDtypeStruct((2, LAYERS, n * CAP, D), BF),
            jax.ShapeDtypeStruct((2, LAYERS, n * CAP, D), F32),
            jax.ShapeDtypeStruct((8 if olds else n, 2, 8, 128), F32),
        ],
        compiler_params=params(),
    )(where, *xs, w, v, *olds)


def composite_kernel(table_ref, slot_ref, gate_ref, delta_ref, target_ref, rend_ref, cot_ref):
    table = jnp.concatenate(
        [
            jnp.concatenate([table_ref[:, c, :], table_ref[:, 4 + c, :]], axis=1)
            for c in range(4)
        ],
        axis=0,
    ).astype(BF)
    slot = slot_ref[...]
    place = lax.broadcasted_iota(I32, (CAP, S), 0)
    expert = lax.broadcasted_iota(I32, (EXPERTS, S), 0)
    hots, members, rows = [], [], []
    for j in range(RAYS):
        at = slot[j : j + 1, :]
        hot = jnp.where((at & (CAP - 1)) == place, 1.0, 0.0).astype(BF)
        member = jnp.where(lax.shift_right_logical(at, 8) == expert, 1.0, 0.0)
        found = dot(table, hot, ((1,), (0,)))
        rows.append(
            [
                jnp.sum(found[c * 16 : c * 16 + 16] * member, axis=0, keepdims=True)
                for c in range(4)
            ]
        )
        hots.append(hot)
        members.append(member)
    raw = [jnp.concatenate([rows[j][c] for j in range(RAYS)], axis=0) for c in range(4)]
    gate = gate_ref[...].astype(F32)
    delta = delta_ref[...]
    gated = [gate * r for r in raw]
    lane_r = lax.broadcasted_iota(I32, (128, 128), 0)
    lane_c = lax.broadcasted_iota(I32, (128, 128), 1)
    earlier = (lane_r < lane_c).astype(F32)
    later = (lane_r > lane_c).astype(F32)
    g0 = gated[0]
    density = jnp.maximum(g0, 0.0) + jnp.log1p(jnp.exp(-jnp.abs(g0)))
    radiance = [jax.nn.sigmoid(g) for g in gated[1:]]
    optical = density * delta
    before = dot(optical, earlier, ((1,), (0,)), precision=lax.Precision.HIGHEST)
    reach = jnp.exp(-before)
    passed = jnp.exp(-optical)
    weight = reach * (1.0 - passed)
    eye = lax.broadcasted_iota(I32, (RAYS, RAYS), 0) == lax.broadcasted_iota(I32, (RAYS, RAYS), 1)
    q = jnp.zeros((RAYS, S), F32)
    grads = [None]
    for c in range(3):
        rendered = jnp.sum(weight * radiance[c], axis=1, keepdims=True)
        goal = jnp.sum(jnp.where(eye, target_ref[c : c + 1, :], 0.0), axis=1, keepdims=True)
        rend_ref[c : c + 1, :] = jnp.sum(jnp.where(eye, rendered, 0.0), axis=0, keepdims=True)
        diff = rendered - goal
        q = q + diff * radiance[c]
        grads.append(diff * weight * radiance[c] * (1.0 - radiance[c]))
    push = dot(q * weight, later, ((1,), (0,)), precision=lax.Precision.HIGHEST)
    grads[0] = (q * reach * passed - push) * delta * jax.nn.sigmoid(g0)
    cots = [(gate * g).astype(BF).astype(F32) for g in grads]
    total = jnp.zeros((64, CAP), F32)
    for j in range(RAYS):
        spread = jnp.concatenate([cots[c][j : j + 1, :] * members[j] for c in range(4)], axis=0)
        total = total + dot(spread.astype(BF), hots[j], ((1,), (1,)))
    for c in range(4):
        cot_ref[:, c, :] = total[c * 16 : c * 16 + 16, :128]
        cot_ref[:, 4 + c, :] = total[c * 16 : c * 16 + 16, 128:]


def composite(table, slot, gate, delta, target):
    return pl.pallas_call(
        composite_kernel,
        out_shape=[
            jax.ShapeDtypeStruct((3, RAYS), F32),
            jax.ShapeDtypeStruct((EXPERTS, 8, 128), F32),
        ],
        compiler_params=params(),
    )(table, slot, gate, delta, target)


def backward_kernel(flip, where_ref, cot_ref, w_ref, v_ref, *refs):
    count = len(GROUPS)
    x_refs, h_refs = refs[:8], refs[8 : 8 + count]
    slope_refs, out_ref = refs[8 + count : 8 + 2 * count], refs[-1]
    e = where_ref[9] ^ flip
    head = v_ref[e, 4:8, :].astype(BF)
    grads, grad_head = [], 0.0
    for (pos, n), h_ref in zip(GROUPS, h_refs):
        parts = []
        for i in range(n):
            one = cot_ref[where_ref[pos + i], e]
            parts += [one[0:4], one[4:8]]
        cot = jnp.concatenate(parts, axis=1).astype(BF)
        grad_head = grad_head + dot(cot, h_ref[e, LAYERS - 1], ((1,), (0,)))
        grads.append(dot(cot, head, ((0,), (0,))))
    shifts = [None] * LAYERS
    for l in range(LAYERS - 1, -1, -1):
        total, shift = 0.0, 0.0
        for g, (pos, n) in enumerate(GROUPS):
            grad_pre = (grads[g] * slope_refs[g][e, l]).astype(BF)
            if l > 0:
                below = h_refs[g][e, l - 1]
            else:
                below = jnp.concatenate([x_refs[pos + i][e] for i in range(n)], axis=0)
            total = total + dot(below, grad_pre, ((0,), (0,)))
            shift = shift + dot(jnp.ones((8, n * CAP), BF), grad_pre, ((1,), (0,)))[0:1]
            if l > 0:
                grads[g] = dot(grad_pre, w_ref[e, l], ((1,), (1,)))
        shifts[l] = shift
        for half in range(2):
            at = (l * 2 + half) * 8
            out_ref[:, at : at + 8, :] = total[:, half * 128 : half * 128 + 128].reshape(32, 8, 128)
    extra = jnp.concatenate(shifts + [grad_head, jnp.zeros((120, D), F32)], axis=0)
    out_ref[:, 64:72, :] = extra.T.reshape(32, 8, 128)


def backward(flip, where, cot, w, v, xs, hs, slopes):
    vmem = pl.BlockSpec(memory_space=pltpu.VMEM)
    return pl.pallas_call(
        partial(backward_kernel, flip),
        in_specs=[pl.BlockSpec(memory_space=pltpu.SMEM)] + [vmem] * (11 + 2 * len(GROUPS)),
        out_shape=jax.ShapeDtypeStruct((32, CH, 128), F32),
        compiler_params=params(),
    )(where, cot, w, v, *xs, *hs, *slopes)


def combine_kernel(own_ref, given_ref, out_ref):
    lane = lax.broadcasted_iota(I32, (1, 1, 128), 2)
    extra = own_ref[:, 64:72, :] + given_ref[:, 64:72, :]
    powers = power_of(jnp.max(jnp.max(jnp.abs(extra), axis=0, keepdims=True), axis=1, keepdims=True))
    extra = extra * jnp.exp2(powers)
    note = jnp.zeros((1, 1, 128), F32)
    for l in range(LAYERS):
        rows = slice(l * 16, l * 16 + 16)
        total = own_ref[:, rows, :] + given_ref[:, rows, :]
        top = jnp.max(jnp.abs(total), axis=0)
        top = jnp.max(jnp.max(top, axis=0, keepdims=True), axis=1, keepdims=True)
        power = power_of(top).reshape(1, 1, 1)
        out_ref[:, rows, :] = total * jnp.exp2(power)
        note = jnp.where(lane == 8 + l, power, note)
    own = pltpu.roll(powers.reshape(1, 128), 16, 1).reshape(1, 1, 128)
    note = jnp.where((lane >= 16) & (lane < 24), own, note)
    out_ref[:, 64:72, :] = jnp.where(lane < 8, extra, note)


def power_of(top):
    return jnp.clip(jnp.floor(13.0 - jnp.log2(jnp.maximum(top, 1e-37))), -120.0, 120.0)


def combine(own, given):
    return pl.pallas_call(
        combine_kernel, out_shape=jax.ShapeDtypeStruct((32, CH, 128), F32), compiler_params=params()
    )(own, given)


def finish_kernel(parts_ref, gw_ref, gb_ref, gh_ref):
    for e in range(2):
        notes = parts_ref[:, e, 64:72, :]
        lane = lax.broadcasted_iota(I32, (1, 1, 128), 2)
        for l in range(LAYERS):
            rows = slice(l * 16, l * 16 + 16)
            total = 0.0
            for j in range(16):
                power = jnp.broadcast_to(notes[j, 0:1, 8 + l : 9 + l], (1, 128))
                total = total + parts_ref[j, e, rows, :] * jnp.exp2(-power)
            gw_ref[e, l] = jnp.concatenate([total[0:8], total[8:16]], axis=1)
        extra = 0.0
        for j in range(16):
            power = pltpu.roll(notes[j], 128 - 16, 1)
            extra = extra + jnp.where(lane[0] < 8, notes[j] * jnp.exp2(-power), 0.0)
        extra = jnp.concatenate([extra, jnp.zeros((120, 128), F32)], axis=0).T
        gb_ref[e] = extra[0:4, 0:8]
        gh_ref[e] = extra[4:8, 0:8]


def finish(parts):
    return pl.pallas_call(
        finish_kernel,
        out_shape=[
            jax.ShapeDtypeStruct((2, LAYERS, 8, D), F32),
            jax.ShapeDtypeStruct((2, LAYERS, 8), F32),
            jax.ShapeDtypeStruct((2, 4, 8), F32),
        ],
        compiler_params=params(),
    )(parts)


def along(x, k):
    return lax.ppermute(x, "z", [(i, (i + k) % 8) for i in range(8)])


def local(features, routes, gate_values, deltas, target, w_hidden, b_hidden, w_head):
    z = lax.axis_index("z").astype(I32)
    core = lax.axis_index("c").astype(I32)
    sources = (z - jnp.array(SHIFTS, I32)) & 7
    where = jnp.concatenate([sources, z.reshape(1), core.reshape(1)])
    x = features.reshape(ROWS, D)
    arrived = {}
    *blocks, slot = pack((2, -2, 1, -1), True, routes.reshape(RAYS, S), x)
    for k, block in zip((2, -2, 1, -1), blocks):
        arrived[k] = along(block, k)
    blocks = pack((3, -3, 4, 0), False, slot, x)
    for k, block in zip((3, -3, 4), blocks):
        arrived[k] = along(block, k)
    arrived[0] = blocks[-1]
    copies = prep(w_hidden, b_hidden, w_head)
    copies, arrived[1], arrived[-1] = lax.optimization_barrier((copies, arrived[1], arrived[-1]))
    gathered = lax.cond(
        core >= 0,
        lambda a: lax.all_to_all(a, ("xy", "c"), 0, 0, tiled=True),
        jnp.zeros_like,
        copies,
    )
    w, v = unpack(gathered)
    xs = [arrived[k] for k in SHIFTS]
    hs, slopes, olds = [], [], []
    for g, (pos, n) in enumerate(GROUPS):
        last = g == len(GROUPS) - 1
        h, slope, out = forward(where, xs[pos : pos + n], w, v, olds if last else [])
        hs.append(h)
        slopes.append(slope)
        olds.append(out)
    table = lax.all_to_all(out, "z", 0, 0, tiled=True)
    rendered, cot = composite(table.reshape(EXPERTS, 8, 128), slot, gate_values, deltas, target)
    cot = lax.all_to_all(cot.reshape(8, 2, 8, 128), "z", 0, 0, tiled=True)
    given = backward(1, where, cot, w, v, xs, hs, slopes)
    given = lax.ppermute(given, "c", [(0, 1), (1, 0)])
    grads = combine(backward(0, where, cot, w, v, xs, hs, slopes), given).astype(jnp.float16)
    parts = lax.all_to_all(grads, ("xy", "c"), 0, 0, tiled=True).astype(F32)
    grad_w, grad_b, grad_h = finish(parts.reshape(16, 2, CH, 128))
    return rendered, grad_w, grad_b, grad_h


def solution(mesh):
    split = Mesh(mesh.devices.reshape(8, 16, 2), ("z", "xy", "c"))
    every = ("z", "xy", "c")
    ray = ("xy", "c")
    in_specs = (
        P(every, None, None),
        P(every, None, None),
        P(every, None),
        P(every, None),
        P(None, every),
        P("z", None, ray, None),
        P("z", None, ray),
        P("z", None, ray),
    )
    out_specs = (P(None, every), P("z", None, ray, None), P("z", None, ray), P("z", None, ray))
    return jax.shard_map(local, mesh=split, in_specs=in_specs, out_specs=out_specs, check_vma=False)
```

```python
from functools import partial

import jax
import jax.numpy as jnp
import numpy as np
from jax import lax
from jax.experimental import pallas as pl
from jax.experimental.pallas import tpu as pltpu
from jax.sharding import Mesh
from jax.sharding import PartitionSpec as P

BF = jnp.bfloat16
F32 = jnp.float32
I32 = jnp.int32
K0 = float(np.sqrt(2.0 / np.pi))
K1 = 0.044715
EXPERTS = 16
CAP = 256
ROWS = 2048
RAYS = 16
S = 128
D = 256
LAYERS = 4
SHIFTS = (0, 1, -1, 2, -2, 3, -3, 4)
GROUPS = ((0, 5), (5, 3))
CH = 72


def dot(a, b, dims, **kw):
    return lax.dot_general(a, b, (dims, ((), ())), preferred_element_type=F32, **kw)


def params(mb=16):
    return pltpu.CompilerParams(vmem_limit_bytes=mb * 2**20)


def prep_kernel(w_ref, b_ref, h_ref, out_ref):
    eye = lax.broadcasted_iota(I32, (8, 128), 0) == lax.broadcasted_iota(I32, (8, 128), 1)
    for e in range(2):
        parts = []
        for l in range(LAYERS):
            rows = w_ref[e, l].astype(F32)
            parts += [rows[:, :128], rows[:, 128:]]
        extra = jnp.concatenate([b_ref[e].astype(F32), h_ref[e].astype(F32)], axis=0)
        parts.append(dot(extra.astype(BF), eye.astype(F32).astype(BF), ((0,), (0,))))
        whole = jnp.concatenate(parts, axis=0).astype(BF)
        for d in range(32):
            out_ref[d, e] = whole


def prep(w, b, h):
    return pl.pallas_call(
        prep_kernel, out_shape=jax.ShapeDtypeStruct((32, 2, CH, 128), BF), compiler_params=params()
    )(w, b, h)


def unpack_kernel(g_ref, w_ref, v_ref):
    for e in range(2):
        for l in range(LAYERS):
            for half in range(2):
                at = (l * 2 + half) * 8
                part = g_ref[:, e, at : at + 8, :].astype(F32).reshape(D, 128)
                w_ref[e, l, :, half * 128 : half * 128 + 128] = (0.5 * part).astype(BF)
        extra = g_ref[:, e, 64:72, :].astype(F32).reshape(D, 128)
        extra = extra.T[0:8]
        v_ref[e] = jnp.concatenate([0.5 * extra[0:4], extra[4:8]], axis=0)


def unpack(gathered):
    return pl.pallas_call(
        unpack_kernel,
        out_shape=[
            jax.ShapeDtypeStruct((2, LAYERS, D, D), BF),
            jax.ShapeDtypeStruct((2, 8, D), F32),
        ],
        compiler_params=params(),
    )(gathered)


def slots_of(route):
    member = jnp.concatenate([(route == e).astype(F32) for e in range(EXPERTS)], axis=0)
    member16 = member.astype(BF)
    row = lax.broadcasted_iota(I32, (256, 256), 0)
    col = lax.broadcasted_iota(I32, (256, 256), 1)
    before = ((row // RAYS == col // RAYS) & (col < row)).astype(F32).astype(BF)
    lane_r = lax.broadcasted_iota(I32, (128, 128), 0)
    lane_c = lax.broadcasted_iota(I32, (128, 128), 1)
    upto = (lane_r <= lane_c).astype(F32).astype(BF)
    within = dot(member16, upto, ((1,), (0,)))
    earlier = dot(before, member16, ((1,), (0,)))
    earlier = dot(earlier.astype(BF), jnp.ones((128, 128), BF), ((1,), (0,)))
    rank = within + earlier - 1.0
    slot = jnp.zeros((RAYS, S), F32)
    for e in range(EXPERTS):
        part = slice(e * RAYS, (e + 1) * RAYS)
        slot = slot + member[part] * (rank[part] + float(e * CAP))
    return slot.astype(I32)


def pack_block(plane, slot_ref, x_ref, out_ref):
    place = lax.broadcasted_iota(I32, (CAP, S), 0)
    for half in range(2):
        base = (plane * 2 + half) * CAP
        hot = jnp.concatenate(
            [
                jnp.where(slot_ref[j : j + 1, :] - base == place, 1.0, 0.0).astype(BF)
                for j in range(RAYS)
            ],
            axis=1,
        )
        out_ref[half] = dot(hot, x_ref[...], ((1,), (0,))).astype(BF)


def pack_kernel(shifts, first, *refs):
    if first:
        route_ref, x_ref, *out_refs, slot_ref = refs
        slot_ref[...] = slots_of(route_ref[...])
    else:
        slot_ref, x_ref, *out_refs = refs
    plane = lax.axis_index("z")
    for k, out_ref in zip(shifts, out_refs):
        pack_block((plane + (k & 7)) & 7, slot_ref, x_ref, out_ref)


def pack(shifts, first, route, x):
    out_shape = [jax.ShapeDtypeStruct((2, CAP, D), BF) for _ in shifts]
    if first:
        out_shape.append(jax.ShapeDtypeStruct((RAYS, S), I32))
    return pl.pallas_call(
        partial(pack_kernel, shifts, first), out_shape=out_shape, compiler_params=params()
    )(route, x)


def forward_kernel(n, olds_n, where_ref, *refs):
    x_refs, (w_ref, v_ref), refs = refs[:n], refs[n : n + 2], refs[n + 2 :]
    olds, (h_ref, slope_ref, out_ref) = refs[:olds_n], refs[olds_n:]
    hidden = [jnp.concatenate([r[e] for r in x_refs], axis=0) for e in range(2)]
    for l in range(LAYERS):
        for e in range(2):
            pre = dot(hidden[e], w_ref[e, l], ((1,), (0,))) + v_ref[e, l : l + 1, :]
            cubic = (8.0 * K0 * K1) * (pre * pre)
            t = jnp.tanh(pre * (2.0 * K0 + cubic))
            twice = 1.0 + t
            value = pre * twice
            slope_ref[e, l] = twice + value * (1.0 - t) * (2.0 * K0 + 3.0 * cubic)
            hidden[e] = value.astype(BF)
            h_ref[e, l] = hidden[e]
    pos = 0
    for old in olds:
        for i in range(old.shape[0]):
            out_ref[where_ref[pos]] = old[i]
            pos += 1
    outs = [dot(v_ref[e].astype(BF), hidden[e], ((1,), (1,)))[4:8] for e in range(2)]
    for i in range(n):
        lo = i * CAP
        one = [out[:, at : at + 128] for out in outs for at in (lo, lo + 128)]
        one = jnp.concatenate(one, axis=0).astype(BF)
        if olds_n:
            out_ref[where_ref[pos + i]] = one
        else:
            out_ref[i] = one


def forward(where, xs, w, v, olds):
    n = len(xs)
    vmem = pl.BlockSpec(memory_space=pltpu.VMEM)
    return pl.pallas_call(
        partial(forward_kernel, n, len(olds)),
        in_specs=[pl.BlockSpec(memory_space=pltpu.SMEM)] + [vmem] * (n + 2 + len(olds)),
        out_shape=[
            jax.ShapeDtypeStruct((2, LAYERS, n * CAP, D), BF),
            jax.ShapeDtypeStruct((2, LAYERS, n * CAP, D), F32),
            jax.ShapeDtypeStruct((8 if olds else n, 16, 128), BF),
        ],
        compiler_params=params(),
    )(where, *xs, w, v, *olds)


def composite_kernel(
    table16_ref, slot_ref, gate_ref, delta_ref, target_ref, rend_ref, cot16_ref, table_ref, cot_ref
):
    table_ref[...] = table16_ref[...].astype(F32).reshape(EXPERTS, 8, 128)
    table = jnp.concatenate(
        [
            jnp.concatenate([table_ref[:, c, :], table_ref[:, 4 + c, :]], axis=1)
            for c in range(4)
        ],
        axis=0,
    ).astype(BF)
    slot = slot_ref[...]
    place = lax.broadcasted_iota(I32, (CAP, S), 0)
    expert = lax.broadcasted_iota(I32, (EXPERTS, S), 0)
    hots, members, rows = [], [], []
    for j in range(RAYS):
        at = slot[j : j + 1, :]
        hot = jnp.where((at & (CAP - 1)) == place, 1.0, 0.0).astype(BF)
        member = jnp.where(lax.shift_right_logical(at, 8) == expert, 1.0, 0.0)
        found = dot(table, hot, ((1,), (0,)))
        rows.append(
            [
                jnp.sum(found[c * 16 : c * 16 + 16] * member, axis=0, keepdims=True)
                for c in range(4)
            ]
        )
        hots.append(hot)
        members.append(member)
    raw = [jnp.concatenate([rows[j][c] for j in range(RAYS)], axis=0) for c in range(4)]
    gate = gate_ref[...].astype(F32)
    delta = delta_ref[...]
    gated = [gate * r for r in raw]
    lane_r = lax.broadcasted_iota(I32, (128, 128), 0)
    lane_c = lax.broadcasted_iota(I32, (128, 128), 1)
    earlier = (lane_r < lane_c).astype(F32)
    later = (lane_r > lane_c).astype(F32)
    g0 = gated[0]
    density = jnp.maximum(g0, 0.0) + jnp.log1p(jnp.exp(-jnp.abs(g0)))
    radiance = [jax.nn.sigmoid(g) for g in gated[1:]]
    optical = density * delta
    before = dot(optical, earlier, ((1,), (0,)), precision=lax.Precision.HIGHEST)
    reach = jnp.exp(-before)
    passed = jnp.exp(-optical)
    weight = reach * (1.0 - passed)
    eye = lax.broadcasted_iota(I32, (RAYS, RAYS), 0) == lax.broadcasted_iota(I32, (RAYS, RAYS), 1)
    q = jnp.zeros((RAYS, S), F32)
    grads = [None]
    for c in range(3):
        rendered = jnp.sum(weight * radiance[c], axis=1, keepdims=True)
        goal = jnp.sum(jnp.where(eye, target_ref[c : c + 1, :], 0.0), axis=1, keepdims=True)
        rend_ref[c : c + 1, :] = jnp.sum(jnp.where(eye, rendered, 0.0), axis=0, keepdims=True)
        diff = rendered - goal
        q = q + diff * radiance[c]
        grads.append(diff * weight * radiance[c] * (1.0 - radiance[c]))
    push = dot(q * weight, later, ((1,), (0,)), precision=lax.Precision.HIGHEST)
    grads[0] = (q * reach * passed - push) * delta * jax.nn.sigmoid(g0)
    cots = [(gate * g).astype(BF).astype(F32) for g in grads]
    total = jnp.zeros((64, CAP), F32)
    for j in range(RAYS):
        spread = jnp.concatenate([cots[c][j : j + 1, :] * members[j] for c in range(4)], axis=0)
        total = total + dot(spread.astype(BF), hots[j], ((1,), (1,)))
    for c in range(4):
        cot_ref[:, c, :] = total[c * 16 : c * 16 + 16, :128]
        cot_ref[:, 4 + c, :] = total[c * 16 : c * 16 + 16, 128:]
    cot16_ref[...] = cot_ref[...].reshape(8, 16, 128).astype(BF)


def composite(table, slot, gate, delta, target):
    return pl.pallas_call(
        composite_kernel,
        out_shape=[
            jax.ShapeDtypeStruct((3, RAYS), F32),
            jax.ShapeDtypeStruct((8, 16, 128), BF),
        ],
        scratch_shapes=[pltpu.VMEM((EXPERTS, 8, 128), F32)] * 2,
        compiler_params=params(),
    )(table, slot, gate, delta, target)


def backward_kernel(flip, where_ref, cot_ref, w_ref, v_ref, *refs):
    count = len(GROUPS)
    x_refs, h_refs = refs[:8], refs[8 : 8 + count]
    slope_refs, out_ref = refs[8 + count : 8 + 2 * count], refs[-1]
    e = where_ref[9] ^ flip
    head = (0.5 * v_ref[e, 4:8, :]).astype(BF)
    grads, grad_head = [], 0.0
    for (pos, n), h_ref in zip(GROUPS, h_refs):
        parts = []
        for i in range(n):
            one = cot_ref[where_ref[pos + i]].astype(F32)
            one = jnp.where(e == 0, one[0:8], one[8:16])
            parts += [one[0:4], one[4:8]]
        cot = jnp.concatenate(parts, axis=1).astype(BF)
        grad_head = grad_head + dot(cot, h_ref[e, LAYERS - 1], ((1,), (0,)))
        grads.append(dot(cot, head, ((0,), (0,))))
    shifts = [None] * LAYERS
    for l in range(LAYERS - 1, -1, -1):
        total, shift = 0.0, 0.0
        for g, (pos, n) in enumerate(GROUPS):
            grad_pre = (grads[g] * slope_refs[g][e, l]).astype(BF)
            if l > 0:
                below = h_refs[g][e, l - 1]
            else:
                below = jnp.concatenate([x_refs[pos + i][e] for i in range(n)], axis=0)
            total = total + dot(below, grad_pre, ((0,), (0,)))
            shift = shift + dot(jnp.ones((8, n * CAP), BF), grad_pre, ((1,), (0,)))[0:1]
            if l > 0:
                grads[g] = dot(grad_pre, w_ref[e, l], ((1,), (1,)))
        shifts[l] = shift
        for half in range(2):
            at = (l * 2 + half) * 8
            out_ref[:, at : at + 8, :] = total[:, half * 128 : half * 128 + 128].reshape(32, 8, 128)
    extra = jnp.concatenate(shifts + [grad_head, jnp.zeros((120, D), F32)], axis=0)
    out_ref[:, 64:72, :] = extra.T.reshape(32, 8, 128)


def backward(flip, where, cot, w, v, xs, hs, slopes):
    vmem = pl.BlockSpec(memory_space=pltpu.VMEM)
    return pl.pallas_call(
        partial(backward_kernel, flip),
        in_specs=[pl.BlockSpec(memory_space=pltpu.SMEM)] + [vmem] * (11 + 2 * len(GROUPS)),
        out_shape=jax.ShapeDtypeStruct((32, CH, 128), F32),
        compiler_params=params(),
    )(where, cot, w, v, *xs, *hs, *slopes)


def combine_kernel(own_ref, given_ref, out_ref):
    lane = lax.broadcasted_iota(I32, (1, 1, 128), 2)
    extra = own_ref[:, 64:72, :] + given_ref[:, 64:72, :]
    powers = power_of(jnp.max(jnp.max(jnp.abs(extra), axis=0, keepdims=True), axis=1, keepdims=True))
    extra = extra * jnp.exp2(powers)
    note = jnp.zeros((1, 1, 128), F32)
    for l in range(LAYERS):
        rows = slice(l * 16, l * 16 + 16)
        total = own_ref[:, rows, :] + given_ref[:, rows, :]
        top = jnp.max(jnp.abs(total), axis=0)
        top = jnp.max(jnp.max(top, axis=0, keepdims=True), axis=1, keepdims=True)
        power = power_of(top).reshape(1, 1, 1)
        out_ref[:, rows, :] = total * jnp.exp2(power)
        note = jnp.where(lane == 8 + l, power, note)
    own = pltpu.roll(powers.reshape(1, 128), 16, 1).reshape(1, 1, 128)
    note = jnp.where((lane >= 16) & (lane < 24), own, note)
    out_ref[:, 64:72, :] = jnp.where(lane < 8, extra, note)


def power_of(top):
    return jnp.clip(jnp.floor(13.0 - jnp.log2(jnp.maximum(top, 1e-37))), -120.0, 120.0)


def combine(own, given):
    return pl.pallas_call(
        combine_kernel, out_shape=jax.ShapeDtypeStruct((32, CH, 128), F32), compiler_params=params()
    )(own, given)


def finish_kernel(parts_ref, gw_ref, gb_ref, gh_ref):
    for e in range(2):
        notes = parts_ref[:, e, 64:72, :]
        lane = lax.broadcasted_iota(I32, (1, 1, 128), 2)
        for l in range(LAYERS):
            rows = slice(l * 16, l * 16 + 16)
            total = 0.0
            for j in range(16):
                power = jnp.broadcast_to(notes[j, 0:1, 8 + l : 9 + l], (1, 128))
                total = total + parts_ref[j, e, rows, :] * jnp.exp2(-power)
            gw_ref[e, l] = jnp.concatenate([total[0:8], total[8:16]], axis=1)
        extra = 0.0
        for j in range(16):
            power = pltpu.roll(notes[j], 128 - 16, 1)
            extra = extra + jnp.where(lane[0] < 8, notes[j] * jnp.exp2(-power), 0.0)
        extra = jnp.concatenate([extra, jnp.zeros((120, 128), F32)], axis=0).T
        gb_ref[e] = extra[0:4, 0:8]
        gh_ref[e] = extra[4:8, 0:8]


def finish(parts):
    return pl.pallas_call(
        finish_kernel,
        out_shape=[
            jax.ShapeDtypeStruct((2, LAYERS, 8, D), F32),
            jax.ShapeDtypeStruct((2, LAYERS, 8), F32),
            jax.ShapeDtypeStruct((2, 4, 8), F32),
        ],
        compiler_params=params(),
    )(parts)


def along(x, k):
    return lax.ppermute(x, "z", [(i, (i + k) % 8) for i in range(8)])


def local(features, routes, gate_values, deltas, target, w_hidden, b_hidden, w_head):
    z = lax.axis_index("z").astype(I32)
    core = lax.axis_index("c").astype(I32)
    sources = (z - jnp.array(SHIFTS, I32)) & 7
    where = jnp.concatenate([sources, z.reshape(1), core.reshape(1)])
    x = features.reshape(ROWS, D)
    arrived = {}
    *blocks, slot = pack((2, -2, 1, -1), True, routes.reshape(RAYS, S), x)
    for k, block in zip((2, -2, 1, -1), blocks):
        arrived[k] = along(block, k)
    blocks = pack((3, -3, 4, 0), False, slot, x)
    for k, block in zip((3, -3, 4), blocks):
        arrived[k] = along(block, k)
    arrived[0] = blocks[-1]
    copies = prep(w_hidden, b_hidden, w_head)
    copies, arrived[1], arrived[-1] = lax.optimization_barrier((copies, arrived[1], arrived[-1]))
    gathered = lax.cond(
        core >= 0,
        lambda a: lax.all_to_all(a, ("xy", "c"), 0, 0, tiled=True),
        jnp.zeros_like,
        copies,
    )
    w, v = unpack(gathered)
    xs = [arrived[k] for k in SHIFTS]
    hs, slopes, olds = [], [], []
    for g, (pos, n) in enumerate(GROUPS):
        last = g == len(GROUPS) - 1
        h, slope, out = forward(where, xs[pos : pos + n], w, v, olds if last else [])
        hs.append(h)
        slopes.append(slope)
        olds.append(out)
    table = lax.all_to_all(out, "z", 0, 0, tiled=True)
    rendered, cot = composite(table, slot, gate_values, deltas, target)
    cot = lax.all_to_all(cot, "z", 0, 0, tiled=True)
    given = backward(1, where, cot, w, v, xs, hs, slopes)
    given = lax.ppermute(given, "c", [(0, 1), (1, 0)])
    grads = combine(backward(0, where, cot, w, v, xs, hs, slopes), given).astype(jnp.float16)
    parts = lax.all_to_all(grads, ("xy", "c"), 0, 0, tiled=True).astype(F32)
    grad_w, grad_b, grad_h = finish(parts.reshape(16, 2, CH, 128))
    return rendered, grad_w, grad_b, grad_h


def solution(mesh):
    split = Mesh(mesh.devices.reshape(8, 16, 2), ("z", "xy", "c"))
    every = ("z", "xy", "c")
    ray = ("xy", "c")
    in_specs = (
        P(every, None, None),
        P(every, None, None),
        P(every, None),
        P(every, None),
        P(None, every),
        P("z", None, ray, None),
        P("z", None, ray),
        P("z", None, ray),
    )
    out_specs = (P(None, every), P("z", None, ray, None), P("z", None, ray), P("z", None, ray))
    return jax.shard_map(local, mesh=split, in_specs=in_specs, out_specs=out_specs, check_vma=False)
```

```python
from functools import partial

import jax
import jax.numpy as jnp
import numpy as np
from jax import lax
from jax.experimental import pallas as pl
from jax.experimental.pallas import tpu as pltpu
from jax.sharding import Mesh
from jax.sharding import PartitionSpec as P

BF = jnp.bfloat16
F32 = jnp.float32
I32 = jnp.int32
K0 = float(np.sqrt(2.0 / np.pi))
K1 = 0.044715
EXPERTS = 16
CAP = 256
ROWS = 2048
RAYS = 16
S = 128
D = 256
LAYERS = 4
SHIFTS = (0, 1, -1, 2, -2, 3, -3, 4)
GROUPS = ((0, 5), (5, 3))
CH = 72


def dot(a, b, dims, **kw):
    return lax.dot_general(a, b, (dims, ((), ())), preferred_element_type=F32, **kw)


def params(mb=16):
    return pltpu.CompilerParams(vmem_limit_bytes=mb * 2**20)


def prep_kernel(w_ref, b_ref, h_ref, out_ref):
    eye = lax.broadcasted_iota(I32, (8, 128), 0) == lax.broadcasted_iota(I32, (8, 128), 1)
    for e in range(2):
        parts = []
        for l in range(LAYERS):
            rows = w_ref[e, l].astype(F32)
            parts += [rows[:, :128], rows[:, 128:]]
        extra = jnp.concatenate([b_ref[e].astype(F32), h_ref[e].astype(F32)], axis=0)
        parts.append(dot(extra.astype(BF), eye.astype(F32).astype(BF), ((0,), (0,))))
        whole = jnp.concatenate(parts, axis=0).astype(BF)
        for d in range(32):
            out_ref[d, e] = whole


def prep(w, b, h):
    return pl.pallas_call(
        prep_kernel, out_shape=jax.ShapeDtypeStruct((32, 2, CH, 128), BF), compiler_params=params()
    )(w, b, h)


def unpack_kernel(g_ref, w_ref, v_ref):
    for e in range(2):
        for l in range(LAYERS):
            for half in range(2):
                at = (l * 2 + half) * 8
                part = g_ref[:, e, at : at + 8, :].astype(F32).reshape(D, 128)
                w_ref[e, l, :, half * 128 : half * 128 + 128] = (0.5 * part).astype(BF)
        extra = g_ref[:, e, 64:72, :].astype(F32).reshape(D, 128)
        extra = extra.T[0:8]
        v_ref[e] = jnp.concatenate([0.5 * extra[0:4], extra[4:8]], axis=0)


def slots_of(route):
    member = jnp.concatenate([(route == e).astype(F32) for e in range(EXPERTS)], axis=0)
    member16 = member.astype(BF)
    row = lax.broadcasted_iota(I32, (256, 256), 0)
    col = lax.broadcasted_iota(I32, (256, 256), 1)
    before = ((row // RAYS == col // RAYS) & (col < row)).astype(F32).astype(BF)
    lane_r = lax.broadcasted_iota(I32, (128, 128), 0)
    lane_c = lax.broadcasted_iota(I32, (128, 128), 1)
    upto = (lane_r <= lane_c).astype(F32).astype(BF)
    within = dot(member16, upto, ((1,), (0,)))
    earlier = dot(before, member16, ((1,), (0,)))
    earlier = dot(earlier.astype(BF), jnp.ones((128, 128), BF), ((1,), (0,)))
    rank = within + earlier - 1.0
    slot = jnp.zeros((RAYS, S), F32)
    for e in range(EXPERTS):
        part = slice(e * RAYS, (e + 1) * RAYS)
        slot = slot + member[part] * (rank[part] + float(e * CAP))
    return slot.astype(I32)


def pack_block(plane, slot_ref, x_ref, out_ref):
    place = lax.broadcasted_iota(I32, (CAP, S), 0)
    for half in range(2):
        base = (plane * 2 + half) * CAP
        hot = jnp.concatenate(
            [
                jnp.where(slot_ref[j : j + 1, :] - base == place, 1.0, 0.0).astype(BF)
                for j in range(RAYS)
            ],
            axis=1,
        )
        out_ref[half] = dot(hot, x_ref[...], ((1,), (0,))).astype(BF)


def pack_kernel(shifts, first, *refs):
    if first:
        route_ref, x_ref, *out_refs, slot_ref = refs
        slot_ref[...] = slots_of(route_ref[...])
    else:
        slot_ref, x_ref, *out_refs = refs
    plane = lax.axis_index("z")
    for k, out_ref in zip(shifts, out_refs):
        pack_block((plane + (k & 7)) & 7, slot_ref, x_ref, out_ref)


def pack(shifts, first, route, x):
    out_shape = [jax.ShapeDtypeStruct((2, CAP, D), BF) for _ in shifts]
    if first:
        out_shape.append(jax.ShapeDtypeStruct((RAYS, S), I32))
    return pl.pallas_call(
        partial(pack_kernel, shifts, first), out_shape=out_shape, compiler_params=params()
    )(route, x)


def forward_kernel(n, olds_n, where_ref, *refs):
    x_refs, refs = refs[:n], refs[n:]
    if olds_n:
        (w_ref, v_ref), olds, (h_ref, slope_ref, out_ref) = refs[:2], refs[2:-3], refs[-3:]
    else:
        g_ref, h_ref, slope_ref, out_ref, w_ref, v_ref = refs
        olds = ()
        unpack_kernel(g_ref, w_ref, v_ref)
    hidden = [jnp.concatenate([r[e] for r in x_refs], axis=0) for e in range(2)]
    for l in range(LAYERS):
        for e in range(2):
            pre = dot(hidden[e], w_ref[e, l], ((1,), (0,))) + v_ref[e, l : l + 1, :]
            cubic = (8.0 * K0 * K1) * (pre * pre)
            t = jnp.tanh(pre * (2.0 * K0 + cubic))
            twice = 1.0 + t
            value = pre * twice
            slope_ref[e, l] = twice + value * (1.0 - t) * (2.0 * K0 + 3.0 * cubic)
            hidden[e] = value.astype(BF)
            h_ref[e, l] = hidden[e]
    pos = 0
    for old in olds:
        for i in range(old.shape[0]):
            out_ref[where_ref[pos]] = old[i]
            pos += 1
    outs = [dot(v_ref[e].astype(BF), hidden[e], ((1,), (1,)))[4:8] for e in range(2)]
    for i in range(n):
        lo = i * CAP
        one = [out[:, at : at + 128] for out in outs for at in (lo, lo + 128)]
        one = jnp.concatenate(one, axis=0).astype(BF)
        if olds_n:
            out_ref[where_ref[pos + i]] = one
        else:
            out_ref[i] = one


def forward(where, xs, weights, olds):
    n = len(xs)
    vmem = pl.BlockSpec(memory_space=pltpu.VMEM)
    out_shape = [
        jax.ShapeDtypeStruct((2, LAYERS, n * CAP, D), BF),
        jax.ShapeDtypeStruct((2, LAYERS, n * CAP, D), F32),
        jax.ShapeDtypeStruct((8 if olds else n, 16, 128), BF),
    ]
    if not olds:
        out_shape.append(jax.ShapeDtypeStruct((2, LAYERS, D, D), BF))
        out_shape.append(jax.ShapeDtypeStruct((2, 8, D), F32))
    count = n + len(weights) + len(olds)
    return pl.pallas_call(
        partial(forward_kernel, n, len(olds)),
        in_specs=[pl.BlockSpec(memory_space=pltpu.SMEM)] + [vmem] * count,
        out_shape=out_shape,
        compiler_params=params(),
    )(where, *xs, *weights, *olds)


def composite_kernel(
    table16_ref, slot_ref, gate_ref, delta_ref, target_ref, rend_ref, cot16_ref, table_ref, cot_ref
):
    table_ref[...] = table16_ref[...].astype(F32).reshape(EXPERTS, 8, 128)
    table = jnp.concatenate(
        [
            jnp.concatenate([table_ref[:, c, :], table_ref[:, 4 + c, :]], axis=1)
            for c in range(4)
        ],
        axis=0,
    ).astype(BF)
    slot = slot_ref[...]
    place = lax.broadcasted_iota(I32, (CAP, S), 0)
    expert = lax.broadcasted_iota(I32, (EXPERTS, S), 0)
    hots, members, rows = [], [], []
    for j in range(RAYS):
        at = slot[j : j + 1, :]
        hot = jnp.where((at & (CAP - 1)) == place, 1.0, 0.0).astype(BF)
        member = jnp.where(lax.shift_right_logical(at, 8) == expert, 1.0, 0.0)
        found = dot(table, hot, ((1,), (0,)))
        rows.append(
            [
                jnp.sum(found[c * 16 : c * 16 + 16] * member, axis=0, keepdims=True)
                for c in range(4)
            ]
        )
        hots.append(hot)
        members.append(member)
    raw = [jnp.concatenate([rows[j][c] for j in range(RAYS)], axis=0) for c in range(4)]
    gate = gate_ref[...].astype(F32)
    delta = delta_ref[...]
    gated = [gate * r for r in raw]
    lane_r = lax.broadcasted_iota(I32, (128, 128), 0)
    lane_c = lax.broadcasted_iota(I32, (128, 128), 1)
    earlier = (lane_r < lane_c).astype(F32)
    later = (lane_r > lane_c).astype(F32)
    g0 = gated[0]
    density = jnp.maximum(g0, 0.0) + jnp.log1p(jnp.exp(-jnp.abs(g0)))
    radiance = [jax.nn.sigmoid(g) for g in gated[1:]]
    optical = density * delta
    before = dot(optical, earlier, ((1,), (0,)), precision=lax.Precision.HIGHEST)
    reach = jnp.exp(-before)
    passed = jnp.exp(-optical)
    weight = reach * (1.0 - passed)
    eye = lax.broadcasted_iota(I32, (RAYS, RAYS), 0) == lax.broadcasted_iota(I32, (RAYS, RAYS), 1)
    q = jnp.zeros((RAYS, S), F32)
    grads = [None]
    for c in range(3):
        rendered = jnp.sum(weight * radiance[c], axis=1, keepdims=True)
        goal = jnp.sum(jnp.where(eye, target_ref[c : c + 1, :], 0.0), axis=1, keepdims=True)
        rend_ref[c : c + 1, :] = jnp.sum(jnp.where(eye, rendered, 0.0), axis=0, keepdims=True)
        diff = rendered - goal
        q = q + diff * radiance[c]
        grads.append(diff * weight * radiance[c] * (1.0 - radiance[c]))
    push = dot(q * weight, later, ((1,), (0,)), precision=lax.Precision.HIGHEST)
    grads[0] = (q * reach * passed - push) * delta * jax.nn.sigmoid(g0)
    cots = [(gate * g).astype(BF).astype(F32) for g in grads]
    total = jnp.zeros((64, CAP), F32)
    for j in range(RAYS):
        spread = jnp.concatenate([cots[c][j : j + 1, :] * members[j] for c in range(4)], axis=0)
        total = total + dot(spread.astype(BF), hots[j], ((1,), (1,)))
    for c in range(4):
        cot_ref[:, c, :] = total[c * 16 : c * 16 + 16, :128]
        cot_ref[:, 4 + c, :] = total[c * 16 : c * 16 + 16, 128:]
    cot16_ref[...] = cot_ref[...].reshape(8, 16, 128).astype(BF)


def composite(table, slot, gate, delta, target):
    return pl.pallas_call(
        composite_kernel,
        out_shape=[
            jax.ShapeDtypeStruct((3, RAYS), F32),
            jax.ShapeDtypeStruct((8, 16, 128), BF),
        ],
        scratch_shapes=[pltpu.VMEM((EXPERTS, 8, 128), F32)] * 2,
        compiler_params=params(),
    )(table, slot, gate, delta, target)


def backward_kernel(flip, where_ref, cot_ref, w_ref, v_ref, *refs):
    count = len(GROUPS)
    x_refs, h_refs = refs[:8], refs[8 : 8 + count]
    slope_refs, out_ref = refs[8 + count : 8 + 2 * count], refs[-1]
    e = where_ref[9] ^ flip
    head = (0.5 * v_ref[e, 4:8, :]).astype(BF)
    grads, grad_head = [], 0.0
    for (pos, n), h_ref in zip(GROUPS, h_refs):
        parts = []
        for i in range(n):
            one = cot_ref[where_ref[pos + i]].astype(F32)
            one = jnp.where(e == 0, one[0:8], one[8:16])
            parts += [one[0:4], one[4:8]]
        cot = jnp.concatenate(parts, axis=1).astype(BF)
        grad_head = grad_head + dot(cot, h_ref[e, LAYERS - 1], ((1,), (0,)))
        grads.append(dot(cot, head, ((0,), (0,))))
    shifts = [None] * LAYERS
    for l in range(LAYERS - 1, -1, -1):
        total, shift = 0.0, 0.0
        for g, (pos, n) in enumerate(GROUPS):
            grad_pre = (grads[g] * slope_refs[g][e, l]).astype(BF)
            if l > 0:
                below = h_refs[g][e, l - 1]
            else:
                below = jnp.concatenate([x_refs[pos + i][e] for i in range(n)], axis=0)
            total = total + dot(below, grad_pre, ((0,), (0,)))
            shift = shift + dot(jnp.ones((8, n * CAP), BF), grad_pre, ((1,), (0,)))[0:1]
            if l > 0:
                grads[g] = dot(grad_pre, w_ref[e, l], ((1,), (1,)))
        shifts[l] = shift
        for half in range(2):
            at = (l * 2 + half) * 8
            out_ref[:, at : at + 8, :] = total[:, half * 128 : half * 128 + 128].reshape(32, 8, 128)
    extra = jnp.concatenate(shifts + [grad_head, jnp.zeros((120, D), F32)], axis=0)
    out_ref[:, 64:72, :] = extra.T.reshape(32, 8, 128)


def backward(flip, where, cot, w, v, xs, hs, slopes):
    vmem = pl.BlockSpec(memory_space=pltpu.VMEM)
    return pl.pallas_call(
        partial(backward_kernel, flip),
        in_specs=[pl.BlockSpec(memory_space=pltpu.SMEM)] + [vmem] * (11 + 2 * len(GROUPS)),
        out_shape=jax.ShapeDtypeStruct((32, CH, 128), F32),
        compiler_params=params(),
    )(where, cot, w, v, *xs, *hs, *slopes)


def combine_kernel(own_ref, given_ref, out_ref):
    lane = lax.broadcasted_iota(I32, (1, 1, 128), 2)
    extra = own_ref[:, 64:72, :] + given_ref[:, 64:72, :]
    powers = power_of(jnp.max(jnp.max(jnp.abs(extra), axis=0, keepdims=True), axis=1, keepdims=True))
    extra = extra * jnp.exp2(powers)
    note = jnp.zeros((1, 1, 128), F32)
    for l in range(LAYERS):
        rows = slice(l * 16, l * 16 + 16)
        total = own_ref[:, rows, :] + given_ref[:, rows, :]
        top = jnp.max(jnp.abs(total), axis=0)
        top = jnp.max(jnp.max(top, axis=0, keepdims=True), axis=1, keepdims=True)
        power = power_of(top).reshape(1, 1, 1)
        out_ref[:, rows, :] = total * jnp.exp2(power)
        note = jnp.where(lane == 8 + l, power, note)
    own = pltpu.roll(powers.reshape(1, 128), 16, 1).reshape(1, 1, 128)
    note = jnp.where((lane >= 16) & (lane < 24), own, note)
    out_ref[:, 64:72, :] = jnp.where(lane < 8, extra, note)


def power_of(top):
    return jnp.clip(jnp.floor(13.0 - jnp.log2(jnp.maximum(top, 1e-37))), -120.0, 120.0)


def combine(own, given):
    return pl.pallas_call(
        combine_kernel, out_shape=jax.ShapeDtypeStruct((32, CH, 128), F32), compiler_params=params()
    )(own, given)


def finish_kernel(parts_ref, gw_ref, gb_ref, gh_ref):
    for e in range(2):
        notes = parts_ref[:, e, 64:72, :]
        lane = lax.broadcasted_iota(I32, (1, 1, 128), 2)
        for l in range(LAYERS):
            rows = slice(l * 16, l * 16 + 16)
            total = 0.0
            for j in range(16):
                power = jnp.broadcast_to(notes[j, 0:1, 8 + l : 9 + l], (1, 128))
                total = total + parts_ref[j, e, rows, :] * jnp.exp2(-power)
            gw_ref[e, l] = jnp.concatenate([total[0:8], total[8:16]], axis=1)
        extra = 0.0
        for j in range(16):
            power = pltpu.roll(notes[j], 128 - 16, 1)
            extra = extra + jnp.where(lane[0] < 8, notes[j] * jnp.exp2(-power), 0.0)
        extra = jnp.concatenate([extra, jnp.zeros((120, 128), F32)], axis=0).T
        gb_ref[e] = extra[0:4, 0:8]
        gh_ref[e] = extra[4:8, 0:8]


def finish(parts):
    return pl.pallas_call(
        finish_kernel,
        out_shape=[
            jax.ShapeDtypeStruct((2, LAYERS, 8, D), F32),
            jax.ShapeDtypeStruct((2, LAYERS, 8), F32),
            jax.ShapeDtypeStruct((2, 4, 8), F32),
        ],
        compiler_params=params(),
    )(parts)


def along(x, k):
    return lax.ppermute(x, "z", [(i, (i + k) % 8) for i in range(8)])


def local(features, routes, gate_values, deltas, target, w_hidden, b_hidden, w_head):
    z = lax.axis_index("z").astype(I32)
    core = lax.axis_index("c").astype(I32)
    sources = (z - jnp.array(SHIFTS, I32)) & 7
    where = jnp.concatenate([sources, z.reshape(1), core.reshape(1)])
    x = features.reshape(ROWS, D)
    arrived = {}
    *blocks, slot = pack((2, -2, 1, -1), True, routes.reshape(RAYS, S), x)
    for k, block in zip((2, -2, 1, -1), blocks):
        arrived[k] = along(block, k)
    blocks = pack((3, -3, 4, 0), False, slot, x)
    for k, block in zip((3, -3, 4), blocks):
        arrived[k] = along(block, k)
    arrived[0] = blocks[-1]
    copies = prep(w_hidden, b_hidden, w_head)
    copies, arrived[1], arrived[-1] = lax.optimization_barrier((copies, arrived[1], arrived[-1]))
    gathered = lax.cond(
        core >= 0,
        lambda a: lax.all_to_all(a, ("xy", "c"), 0, 0, tiled=True),
        jnp.zeros_like,
        copies,
    )
    xs = [arrived[k] for k in SHIFTS]
    (pos, n), (pos2, n2) = GROUPS
    h, slope, out, w, v = forward(where, xs[pos : pos + n], (gathered,), [])
    h2, slope2, out = forward(where, xs[pos2 : pos2 + n2], (w, v), [out])
    hs, slopes = (h, h2), (slope, slope2)
    table = lax.all_to_all(out, "z", 0, 0, tiled=True)
    rendered, cot = composite(table, slot, gate_values, deltas, target)
    cot = lax.all_to_all(cot, "z", 0, 0, tiled=True)
    given = backward(1, where, cot, w, v, xs, hs, slopes)
    given = lax.ppermute(given, "c", [(0, 1), (1, 0)])
    grads = combine(backward(0, where, cot, w, v, xs, hs, slopes), given).astype(jnp.float16)
    parts = lax.all_to_all(grads, ("xy", "c"), 0, 0, tiled=True).astype(F32)
    grad_w, grad_b, grad_h = finish(parts.reshape(16, 2, CH, 128))
    return rendered, grad_w, grad_b, grad_h


def solution(mesh):
    split = Mesh(mesh.devices.reshape(8, 16, 2), ("z", "xy", "c"))
    every = ("z", "xy", "c")
    ray = ("xy", "c")
    in_specs = (
        P(every, None, None),
        P(every, None, None),
        P(every, None),
        P(every, None),
        P(None, every),
        P("z", None, ray, None),
        P("z", None, ray),
        P("z", None, ray),
    )
    out_specs = (P(None, every), P("z", None, ray, None), P("z", None, ray), P("z", None, ray))
    return jax.shard_map(local, mesh=split, in_specs=in_specs, out_specs=out_specs, check_vma=False)
```

```python
from functools import partial

import jax
import jax.numpy as jnp
import numpy as np
from jax import lax
from jax.experimental import pallas as pl
from jax.experimental.pallas import tpu as pltpu
from jax.sharding import Mesh
from jax.sharding import PartitionSpec as P

BF = jnp.bfloat16
F32 = jnp.float32
I32 = jnp.int32
K0 = float(np.sqrt(2.0 / np.pi))
K1 = 0.044715
EXPERTS = 16
CAP = 256
ROWS = 2048
RAYS = 16
S = 128
D = 256
LAYERS = 4
SHIFTS = (0, 1, -1, 2, -2, 3, -3, 4)
GROUPS = ((0, 5), (5, 3))
CH = 72


def dot(a, b, dims, **kw):
    return lax.dot_general(a, b, (dims, ((), ())), preferred_element_type=F32, **kw)


def params(mb=16):
    return pltpu.CompilerParams(vmem_limit_bytes=mb * 2**20)


def prep_kernel(w_ref, b_ref, h_ref, out_ref):
    eye = lax.broadcasted_iota(I32, (8, 128), 0) == lax.broadcasted_iota(I32, (8, 128), 1)
    for e in range(2):
        parts = []
        for l in range(LAYERS):
            rows = w_ref[e, l].astype(F32)
            parts += [rows[:, :128], rows[:, 128:]]
        extra = jnp.concatenate([b_ref[e].astype(F32), h_ref[e].astype(F32)], axis=0)
        parts.append(dot(extra.astype(BF), eye.astype(F32).astype(BF), ((0,), (0,))))
        whole = jnp.concatenate(parts, axis=0).astype(BF)
        for d in range(32):
            out_ref[d, e] = whole


def prep(w, b, h):
    return pl.pallas_call(
        prep_kernel, out_shape=jax.ShapeDtypeStruct((32, 2, CH, 128), BF), compiler_params=params()
    )(w, b, h)


def unpack_kernel(g_ref, w_ref, v_ref):
    for e in range(2):
        for l in range(LAYERS):
            for half in range(2):
                at = (l * 2 + half) * 8
                part = g_ref[:, e, at : at + 8, :].astype(F32).reshape(D, 128)
                w_ref[e, l, :, half * 128 : half * 128 + 128] = (0.5 * part).astype(BF)
        extra = g_ref[:, e, 64:72, :].astype(F32).reshape(D, 128)
        extra = extra.T[0:8]
        v_ref[e] = jnp.concatenate([0.5 * extra[0:4], extra[4:8]], axis=0)


def slots_of(route):
    member = jnp.concatenate([(route == e).astype(F32) for e in range(EXPERTS)], axis=0)
    member16 = member.astype(BF)
    row = lax.broadcasted_iota(I32, (256, 256), 0)
    col = lax.broadcasted_iota(I32, (256, 256), 1)
    before = ((row // RAYS == col // RAYS) & (col < row)).astype(F32).astype(BF)
    lane_r = lax.broadcasted_iota(I32, (128, 128), 0)
    lane_c = lax.broadcasted_iota(I32, (128, 128), 1)
    upto = (lane_r <= lane_c).astype(F32).astype(BF)
    within = dot(member16, upto, ((1,), (0,)))
    earlier = dot(before, member16, ((1,), (0,)))
    earlier = dot(earlier.astype(BF), jnp.ones((128, 128), BF), ((1,), (0,)))
    rank = within + earlier - 1.0
    slot = jnp.zeros((RAYS, S), F32)
    for e in range(EXPERTS):
        part = slice(e * RAYS, (e + 1) * RAYS)
        slot = slot + member[part] * (rank[part] + float(e * CAP))
    return slot.astype(I32)


def pack_block(plane, slot_ref, x_ref, out_ref):
    place = lax.broadcasted_iota(I32, (CAP, S), 0)
    for half in range(2):
        base = (plane * 2 + half) * CAP
        hot = jnp.concatenate(
            [
                jnp.where(slot_ref[j : j + 1, :] - base == place, 1.0, 0.0).astype(BF)
                for j in range(RAYS)
            ],
            axis=1,
        )
        out_ref[half] = dot(hot, x_ref[...], ((1,), (0,))).astype(BF)


def pack_kernel(shifts, first, *refs):
    if first:
        route_ref, x_ref, *out_refs, slot_ref = refs
        slot_ref[...] = slots_of(route_ref[...])
    else:
        slot_ref, x_ref, *out_refs = refs
    plane = lax.axis_index("z")
    for k, out_ref in zip(shifts, out_refs):
        pack_block((plane + (k & 7)) & 7, slot_ref, x_ref, out_ref)


def pack(shifts, first, route, x):
    out_shape = [jax.ShapeDtypeStruct((2, CAP, D), BF) for _ in shifts]
    if first:
        out_shape.append(jax.ShapeDtypeStruct((RAYS, S), I32))
    return pl.pallas_call(
        partial(pack_kernel, shifts, first), out_shape=out_shape, compiler_params=params()
    )(route, x)


def forward_kernel(n, olds_n, where_ref, *refs):
    x_refs, refs = refs[:n], refs[n:]
    if olds_n:
        (w_ref, v_ref), olds, (h_ref, slope_ref, out_ref) = refs[:2], refs[2:-3], refs[-3:]
    else:
        g_ref, h_ref, slope_ref, out_ref, w_ref, v_ref = refs
        olds = ()
        unpack_kernel(g_ref, w_ref, v_ref)
    hidden = [jnp.concatenate([r[e] for r in x_refs], axis=0) for e in range(2)]
    for l in range(LAYERS):
        for e in range(2):
            pre = dot(hidden[e], w_ref[e, l], ((1,), (0,))) + v_ref[e, l : l + 1, :]
            cubic = (8.0 * K0 * K1) * (pre * pre)
            t = jnp.tanh(pre * (2.0 * K0 + cubic))
            twice = 1.0 + t
            value = pre * twice
            slope_ref[e, l] = twice + value * (1.0 - t) * (2.0 * K0 + 3.0 * cubic)
            hidden[e] = value.astype(BF)
            h_ref[e, l] = hidden[e]
    pos = 0
    for old in olds:
        for i in range(old.shape[0]):
            out_ref[where_ref[pos]] = old[i]
            pos += 1
    outs = [dot(v_ref[e].astype(BF), hidden[e], ((1,), (1,)))[4:8] for e in range(2)]
    for i in range(n):
        lo = i * CAP
        one = [out[:, at : at + 128] for out in outs for at in (lo, lo + 128)]
        one = jnp.concatenate(one, axis=0).astype(BF)
        if olds_n:
            out_ref[where_ref[pos + i]] = one
        else:
            out_ref[i] = one


def forward(where, xs, weights, olds):
    n = len(xs)
    vmem = pl.BlockSpec(memory_space=pltpu.VMEM)
    out_shape = [
        jax.ShapeDtypeStruct((2, LAYERS, n * CAP, D), BF),
        jax.ShapeDtypeStruct((2, LAYERS, n * CAP, D), F32),
        jax.ShapeDtypeStruct((8 if olds else n, 16, 128), BF),
    ]
    if not olds:
        out_shape.append(jax.ShapeDtypeStruct((2, LAYERS, D, D), BF))
        out_shape.append(jax.ShapeDtypeStruct((2, 8, D), F32))
    count = n + len(weights) + len(olds)
    return pl.pallas_call(
        partial(forward_kernel, n, len(olds)),
        in_specs=[pl.BlockSpec(memory_space=pltpu.SMEM)] + [vmem] * count,
        out_shape=out_shape,
        compiler_params=params(),
    )(where, *xs, *weights, *olds)


def composite_kernel(
    table16_ref, slot_ref, gate_ref, delta_ref, target_ref, rend_ref, cot16_ref, table_ref, cot_ref
):
    table_ref[...] = table16_ref[...].astype(F32).reshape(EXPERTS, 8, 128)
    table = jnp.concatenate(
        [
            jnp.concatenate([table_ref[:, c, :], table_ref[:, 4 + c, :]], axis=1)
            for c in range(4)
        ],
        axis=0,
    ).astype(BF)
    slot = slot_ref[...]
    place = lax.broadcasted_iota(I32, (CAP, S), 0)
    expert = lax.broadcasted_iota(I32, (EXPERTS, S), 0)
    hots, members, rows = [], [], []
    for j in range(RAYS):
        at = slot[j : j + 1, :]
        hot = jnp.where((at & (CAP - 1)) == place, 1.0, 0.0).astype(BF)
        member = jnp.where(lax.shift_right_logical(at, 8) == expert, 1.0, 0.0)
        found = dot(table, hot, ((1,), (0,)))
        rows.append(
            [
                jnp.sum(found[c * 16 : c * 16 + 16] * member, axis=0, keepdims=True)
                for c in range(4)
            ]
        )
        hots.append(hot)
        members.append(member)
    raw = [jnp.concatenate([rows[j][c] for j in range(RAYS)], axis=0) for c in range(4)]
    gate = gate_ref[...].astype(F32)
    delta = delta_ref[...]
    gated = [gate * r for r in raw]
    lane_r = lax.broadcasted_iota(I32, (128, 128), 0)
    lane_c = lax.broadcasted_iota(I32, (128, 128), 1)
    earlier = (lane_r < lane_c).astype(F32)
    later = (lane_r > lane_c).astype(F32)
    g0 = gated[0]
    density = jnp.maximum(g0, 0.0) + jnp.log1p(jnp.exp(-jnp.abs(g0)))
    radiance = [jax.nn.sigmoid(g) for g in gated[1:]]
    optical = density * delta
    before = dot(optical, earlier, ((1,), (0,)), precision=lax.Precision.HIGHEST)
    reach = jnp.exp(-before)
    passed = jnp.exp(-optical)
    weight = reach * (1.0 - passed)
    eye = lax.broadcasted_iota(I32, (RAYS, RAYS), 0) == lax.broadcasted_iota(I32, (RAYS, RAYS), 1)
    q = jnp.zeros((RAYS, S), F32)
    grads = [None]
    for c in range(3):
        rendered = jnp.sum(weight * radiance[c], axis=1, keepdims=True)
        goal = jnp.sum(jnp.where(eye, target_ref[c : c + 1, :], 0.0), axis=1, keepdims=True)
        rend_ref[c : c + 1, :] = jnp.sum(jnp.where(eye, rendered, 0.0), axis=0, keepdims=True)
        diff = rendered - goal
        q = q + diff * radiance[c]
        grads.append(diff * weight * radiance[c] * (1.0 - radiance[c]))
    push = dot(q * weight, later, ((1,), (0,)), precision=lax.Precision.HIGHEST)
    grads[0] = (q * reach * passed - push) * delta * jax.nn.sigmoid(g0)
    cots = [(gate * g).astype(BF).astype(F32) for g in grads]
    total = jnp.zeros((64, CAP), F32)
    for j in range(RAYS):
        spread = jnp.concatenate([cots[c][j : j + 1, :] * members[j] for c in range(4)], axis=0)
        total = total + dot(spread.astype(BF), hots[j], ((1,), (1,)))
    for c in range(4):
        cot_ref[:, c, :] = total[c * 16 : c * 16 + 16, :128]
        cot_ref[:, 4 + c, :] = total[c * 16 : c * 16 + 16, 128:]
    cot16_ref[...] = cot_ref[...].reshape(8, 16, 128).astype(BF)


def composite(table, slot, gate, delta, target):
    return pl.pallas_call(
        composite_kernel,
        out_shape=[
            jax.ShapeDtypeStruct((3, RAYS), F32),
            jax.ShapeDtypeStruct((8, 16, 128), BF),
        ],
        scratch_shapes=[pltpu.VMEM((EXPERTS, 8, 128), F32)] * 2,
        compiler_params=params(),
    )(table, slot, gate, delta, target)


def backward_kernel(flip, where_ref, cot_ref, w_ref, v_ref, *refs):
    count = len(GROUPS)
    x_refs, h_refs = refs[:8], refs[8 : 8 + count]
    slope_refs, out_ref = refs[8 + count : 8 + 2 * count], refs[-1]
    e = where_ref[9] ^ flip
    head = (0.5 * v_ref[e, 4:8, :]).astype(BF)
    grads, grad_head = [], 0.0
    for (pos, n), h_ref in zip(GROUPS, h_refs):
        parts = []
        for i in range(n):
            one = cot_ref[where_ref[pos + i]].astype(F32)
            one = jnp.where(e == 0, one[0:8], one[8:16])
            parts += [one[0:4], one[4:8]]
        cot = jnp.concatenate(parts, axis=1).astype(BF)
        grad_head = grad_head + dot(cot, h_ref[e, LAYERS - 1], ((1,), (0,)))
        grads.append(dot(cot, head, ((0,), (0,))))
    shifts = [None] * LAYERS
    for l in range(LAYERS - 1, -1, -1):
        total, shift = 0.0, 0.0
        for g, (pos, n) in enumerate(GROUPS):
            grad_pre = (grads[g] * slope_refs[g][e, l]).astype(BF)
            if l > 0:
                below = h_refs[g][e, l - 1]
            else:
                below = jnp.concatenate([x_refs[pos + i][e] for i in range(n)], axis=0)
            total = total + dot(below, grad_pre, ((0,), (0,)))
            shift = shift + jnp.sum(grad_pre.astype(F32), axis=0, keepdims=True)
            if l > 0:
                grads[g] = dot(grad_pre, w_ref[e, l], ((1,), (1,)))
        shifts[l] = shift
        for half in range(2):
            at = (l * 2 + half) * 8
            out_ref[:, at : at + 8, :] = total[:, half * 128 : half * 128 + 128].reshape(32, 8, 128)
    extra = jnp.concatenate(shifts + [grad_head, jnp.zeros((120, D), F32)], axis=0)
    out_ref[:, 64:72, :] = extra.T.reshape(32, 8, 128)


def backward(flip, where, cot, w, v, xs, hs, slopes):
    vmem = pl.BlockSpec(memory_space=pltpu.VMEM)
    return pl.pallas_call(
        partial(backward_kernel, flip),
        in_specs=[pl.BlockSpec(memory_space=pltpu.SMEM)] + [vmem] * (11 + 2 * len(GROUPS)),
        out_shape=jax.ShapeDtypeStruct((32, CH, 128), F32),
        compiler_params=params(),
    )(where, cot, w, v, *xs, *hs, *slopes)


def combine_kernel(own_ref, given_ref, out_ref):
    lane = lax.broadcasted_iota(I32, (1, 1, 128), 2)
    extra = own_ref[:, 64:72, :] + given_ref[:, 64:72, :]
    powers = power_of(jnp.max(jnp.max(jnp.abs(extra), axis=0, keepdims=True), axis=1, keepdims=True))
    extra = extra * jnp.exp2(powers)
    note = jnp.zeros((1, 1, 128), F32)
    for l in range(LAYERS):
        rows = slice(l * 16, l * 16 + 16)
        total = own_ref[:, rows, :] + given_ref[:, rows, :]
        top = jnp.max(jnp.abs(total), axis=0)
        top = jnp.max(jnp.max(top, axis=0, keepdims=True), axis=1, keepdims=True)
        power = power_of(top).reshape(1, 1, 1)
        out_ref[:, rows, :] = total * jnp.exp2(power)
        note = jnp.where(lane == 8 + l, power, note)
    own = pltpu.roll(powers.reshape(1, 128), 16, 1).reshape(1, 1, 128)
    note = jnp.where((lane >= 16) & (lane < 24), own, note)
    out_ref[:, 64:72, :] = jnp.where(lane < 8, extra, note)


def power_of(top):
    return jnp.clip(jnp.floor(13.0 - jnp.log2(jnp.maximum(top, 1e-37))), -120.0, 120.0)


def combine(own, given):
    return pl.pallas_call(
        combine_kernel, out_shape=jax.ShapeDtypeStruct((32, CH, 128), F32), compiler_params=params()
    )(own, given)


def finish_kernel(parts_ref, gw_ref, gb_ref, gh_ref):
    for e in range(2):
        notes = parts_ref[:, e, 64:72, :]
        lane = lax.broadcasted_iota(I32, (1, 1, 128), 2)
        for l in range(LAYERS):
            rows = slice(l * 16, l * 16 + 16)
            total = 0.0
            for j in range(16):
                power = jnp.broadcast_to(notes[j, 0:1, 8 + l : 9 + l], (1, 128))
                total = total + parts_ref[j, e, rows, :] * jnp.exp2(-power)
            gw_ref[e, l] = jnp.concatenate([total[0:8], total[8:16]], axis=1)
        extra = 0.0
        for j in range(16):
            power = pltpu.roll(notes[j], 128 - 16, 1)
            extra = extra + jnp.where(lane[0] < 8, notes[j] * jnp.exp2(-power), 0.0)
        extra = jnp.concatenate([extra, jnp.zeros((120, 128), F32)], axis=0).T
        gb_ref[e] = extra[0:4, 0:8]
        gh_ref[e] = extra[4:8, 0:8]


def finish(parts):
    return pl.pallas_call(
        finish_kernel,
        out_shape=[
            jax.ShapeDtypeStruct((2, LAYERS, 8, D), F32),
            jax.ShapeDtypeStruct((2, LAYERS, 8), F32),
            jax.ShapeDtypeStruct((2, 4, 8), F32),
        ],
        compiler_params=params(),
    )(parts)


def along(x, k):
    return lax.ppermute(x, "z", [(i, (i + k) % 8) for i in range(8)])


def local(features, routes, gate_values, deltas, target, w_hidden, b_hidden, w_head):
    z = lax.axis_index("z").astype(I32)
    core = lax.axis_index("c").astype(I32)
    sources = (z - jnp.array(SHIFTS, I32)) & 7
    where = jnp.concatenate([sources, z.reshape(1), core.reshape(1)])
    x = features.reshape(ROWS, D)
    arrived = {}
    *blocks, slot = pack((2, -2, 1, -1), True, routes.reshape(RAYS, S), x)
    for k, block in zip((2, -2, 1, -1), blocks):
        arrived[k] = along(block, k)
    blocks = pack((3, -3, 4, 0), False, slot, x)
    for k, block in zip((3, -3, 4), blocks):
        arrived[k] = along(block, k)
    arrived[0] = blocks[-1]
    copies = prep(w_hidden, b_hidden, w_head)
    copies, arrived[1], arrived[-1] = lax.optimization_barrier((copies, arrived[1], arrived[-1]))
    gathered = lax.cond(
        core >= 0,
        lambda a: lax.all_to_all(a, ("xy", "c"), 0, 0, tiled=True),
        jnp.zeros_like,
        copies,
    )
    xs = [arrived[k] for k in SHIFTS]
    (pos, n), (pos2, n2) = GROUPS
    h, slope, out, w, v = forward(where, xs[pos : pos + n], (gathered,), [])
    h2, slope2, out = forward(where, xs[pos2 : pos2 + n2], (w, v), [out])
    hs, slopes = (h, h2), (slope, slope2)
    table = lax.all_to_all(out, "z", 0, 0, tiled=True)
    rendered, cot = composite(table, slot, gate_values, deltas, target)
    cot = lax.all_to_all(cot, "z", 0, 0, tiled=True)
    given = backward(1, where, cot, w, v, xs, hs, slopes)
    given = lax.ppermute(given, "c", [(0, 1), (1, 0)])
    grads = combine(backward(0, where, cot, w, v, xs, hs, slopes), given).astype(jnp.float16)
    parts = lax.all_to_all(grads, ("xy", "c"), 0, 0, tiled=True).astype(F32)
    grad_w, grad_b, grad_h = finish(parts.reshape(16, 2, CH, 128))
    return rendered, grad_w, grad_b, grad_h


def solution(mesh):
    split = Mesh(mesh.devices.reshape(8, 16, 2), ("z", "xy", "c"))
    every = ("z", "xy", "c")
    ray = ("xy", "c")
    in_specs = (
        P(every, None, None),
        P(every, None, None),
        P(every, None),
        P(every, None),
        P(None, every),
        P("z", None, ray, None),
        P("z", None, ray),
        P("z", None, ray),
    )
    out_specs = (P(None, every), P("z", None, ray, None), P("z", None, ray), P("z", None, ray))
    return jax.shard_map(local, mesh=split, in_specs=in_specs, out_specs=out_specs, check_vma=False)
```
